32 devices in a mesh: groups: 1, expert: 32 (over z, y, x, core), cuts: 1.
Axes of the slice: x: 2, y: 2, z: 4, core: 2. Of those that a mesh axis runs over, the one named last changes fastest.
Arguments:
- tokens: bfloat16 [512, 2048], P(('groups', 'expert', 'cuts')), may hold values from -6 to 6
- routes: int32 [512, 8], P(('groups', 'expert', 'cuts')), may hold values from 0 to 31, all different within a row; in each aligned block of 16 rows (0 to 15, 16 to 31, ...) at most 8 rows name the same one
- gate_values: bfloat16 [512, 8], P(('groups', 'expert', 'cuts')), may hold values from 0.049804688 to 1
- expert_in: bfloat16 [32, 2048, 768], P('expert', None, 'cuts'), may hold values from -0.125 to 0.125
- expert_out: bfloat16 [32, 768, 2048], P('expert', 'cuts'), may hold values from -0.21875 to 0.21875
- queries: bfloat16 [32, 8192], P(('groups', 'expert')), may hold values from -4.5 to 4.5
- cached_keys: bfloat16 [32, 1536, 512], P(('groups', 'expert'), 'cuts'), may hold values from -4.5 to 4.5
- cached_values: bfloat16 [32, 1536, 512], P(('groups', 'expert'), 'cuts'), may hold values from -6 to 6
- lengths: int32 [32], P(('groups', 'expert')), may hold values from 1 to 1536, as said below
Outputs:
- moe_out: bfloat16 [512, 2048], P(('groups', 'expert', 'cuts'))
- attention_out: bfloat16 [32, 8192], P(('groups', 'expert'))
The draws below stay inside these ranges and needn't reach their ends.
Inputs may be any that keep to these rules, and one draw needn't show every extreme that they name: `routes`: each row names 8 different experts. In each aligned block of 16 rows (the rows of one device) no expert is named by more than 8 rows, a bound that some block reaches. `lengths`: within each group, some sequence has exactly 1536 live positions.
All inputs are finite; a program needn't handle non-finite values.
Results may differ from the reference program's by a relative error of at most 0.0057.
Values may be sent and summed in bfloat16 or wider, within the bound.
No kernel may reach another device: no remote copies, remote signals or barrier semaphores. Data moves between devices by JAX's collectives and lax.ppermute only.
A program may use at most 64 MiB of HBM per device.

```python
import math
import jax
import jax.numpy as jnp
import numpy as np
from jax import lax

D = 2048
FF = 768
QH = 64
KVH = 4
HD = 128
TOP = 8
TOK_DEV = 16
POS = 1536
EXPERTS = 32
CAP = 8
TOKENS = 512
SEQS = 32


def draw_queries(key, part):
    key = jax.random.fold_in(key, 11)
    base = jnp.clip(jax.random.normal(key, (SEQS, QH, HD), jnp.float32), -4.5, 4.5)
    return base.reshape(SEQS, QH * HD).astype(jnp.bfloat16)


def draw_cached_keys(key, part):
    key = jax.random.fold_in(key, 23)
    base = jnp.clip(jax.random.normal(key, (SEQS, POS, KVH, HD), jnp.float32), -4.5, 4.5)
    return base.reshape(SEQS, POS, KVH * HD).astype(jnp.bfloat16)


def draw_lengths(key, part):
    key = jax.random.fold_in(key, 37)
    first_key, second_key = jax.random.split(key)
    values = jax.random.randint(first_key, (SEQS,), 1, POS + 1, dtype=jnp.int32)
    longest = jax.random.randint(second_key, (), 0, SEQS, dtype=jnp.int32)
    return jnp.where(jnp.arange(SEQS, dtype=jnp.int32) == longest, jnp.int32(POS), values).astype(jnp.int32)


def block_levels(key, dims, pieces, low, largest):
    loudness = 1.0
    for dim, shards_of in pieces:
        heights = jax.random.uniform(jax.random.fold_in(jax.random.fold_in(key, 6), dim), (shards_of,), jnp.float32, low / len(pieces), largest / len(pieces))
        loudness = loudness * jnp.repeat(jnp.exp(heights), dims[dim] // shards_of).reshape((-1,) + (1,) * (len(dims) - 1 - dim))
    return loudness


def assign_block(own_key, own, number, rows, count, top, bound, slope):
    ranking = jax.random.permutation(own_key, count)
    packed, ordinary = shares(count, rows * top, bound, slope, True), shares(count, rows * top, bound, slope, False)
    places = jnp.arange(count)

    def named(tallies, rotation):
        used = int((tallies > 0).sum())
        fixed = max(1, used // 4)
        moved = fixed + (places - fixed + rotation * (used - fixed)) % max(1, count - fixed)
        return jnp.zeros((count,), jnp.int32).at[ranking[jnp.where(places < fixed, places, moved)]].set(jnp.asarray(tallies, jnp.int32))

    tallies = jnp.where(number % 4 == 0, named(packed, number // 4), named(ordinary, number - number // 4 - 1))
    mixed = jax.random.permutation(jax.random.fold_in(own, 3), count)
    giver, taker = mixed[0:count // 2 * 2:2], mixed[1:count // 2 * 2:2]
    slack = jnp.minimum(tallies[giver] - 1, bound - tallies[taker]) // 2
    slack = jnp.where((giver == ranking[0]) | (taker == ranking[0]) | (tallies[taker] == 0), 0, jnp.maximum(slack, 0))
    moved = jax.random.randint(jax.random.fold_in(own, 4), (count // 2,), 0, 1 << 20) % (slack + 1)
    tallies = tallies.at[giver].add(-moved).at[taker].add(moved)
    labels = jnp.searchsorted(jnp.cumsum(tallies), jnp.arange(rows * top), side="right").astype(jnp.int32)
    grid = labels.reshape(top, rows).T
    grid = grid[jax.random.permutation(jax.random.fold_in(own, 1), rows)]
    rotation = jax.random.randint(jax.random.fold_in(own, 2), (rows, 1), 0, top)
    return jnp.take_along_axis(grid, (jnp.arange(top)[None, :] + rotation) % top, axis=1)


def shares(number_of, total, bound, slope, full):
    loads = [(1 << 20) // math.isqrt(standing ** slope) + 1 for standing in range(1, number_of + 1)]
    largest = bound if full else min(bound, max(-(-total // number_of), total * loads[0] // sum(loads)))
    least = 1 if total - largest >= number_of - 1 else 0
    holding, spare = [largest] + [least] * (number_of - 1), total - largest - least * (number_of - 1)
    while spare > 0:
        free = [i for i in range(1, number_of) if holding[i] < largest] or [i for i in range(1, number_of) if holding[i] < bound]
        mass, budget = sum([loads[i] for i in free]), spare
        for i in free:
            addition = min(bound - holding[i], max(1, budget * loads[i] // mass), spare)
            holding[i] = holding[i] + addition
            spare = spare - addition
    return np.array(holding)


def scatter_about(own_key, extent, deviation, most, shards=(), kind=jnp.bfloat16):
    values = jax.random.normal(own_key, extent, jnp.float32) * deviation
    if len(shards) > 0:
        values = block_levels(own_key, extent, shards, -0.22, 0.18) * values
    return jnp.clip(values, min=-most, max=most).astype(kind)


def setup_inputs(seed: int = 0, part: int = 0) -> dict:
    seeds = jax.random.split(jax.random.key(seed), 10)
    own_keys = jax.random.split(jax.random.fold_in(seeds[9], part), 10)
    tokens = scatter_about(own_keys[0], (TOKENS, D), 1.0, 6.0, ((0, 32),))
    routes_keys = jax.random.split(jax.random.fold_in(own_keys[1], 1), TOKENS // TOK_DEV)
    routes_turns = jax.random.permutation(jax.random.fold_in(own_keys[1], 3), TOKENS // TOK_DEV)
    routes = jax.vmap(lambda own, number: assign_block(jax.random.fold_in(own_keys[1], 2), own, number, TOK_DEV, EXPERTS, TOP, CAP, 2))(routes_keys, routes_turns).reshape((TOKENS, TOP))
    gate_values = jnp.clip(jnp.exp(math.log(1.0) - 2.9996462 * jax.random.uniform(own_keys[2], (TOKENS, TOP), jnp.float32) ** block_levels(own_keys[2], (TOKENS, TOP), ((0, 32),), -0.2, 0.2)), 0.049804688, 1.0).astype(jnp.bfloat16)
    expert_in = scatter_about(seeds[3], (EXPERTS, D, FF), D ** -0.5, 0.125, ((0, 32),))
    expert_out = scatter_about(seeds[4], (EXPERTS, FF, D), FF ** -0.5, 0.21875, ((0, 32),))
    queries = draw_queries(jax.random.fold_in(jax.random.fold_in(seeds[9], part), 71), part)
    cached_keys = draw_cached_keys(jax.random.fold_in(jax.random.fold_in(seeds[9], part), 71), part)
    cached_values = scatter_about(own_keys[7], (SEQS, POS, KVH * HD), 1.0, 6.0, ((0, 32),))
    lengths = draw_lengths(jax.random.fold_in(jax.random.fold_in(seeds[9], part), 71), part)
    return dict(tokens=tokens, routes=routes, gate_values=gate_values, expert_in=expert_in, expert_out=expert_out, queries=queries, cached_keys=cached_keys, cached_values=cached_values, lengths=lengths)


def attend(queries, cached_keys, cached_values, lengths):
    seq_count = queries.shape[0]
    group = QH // KVH
    query_f = queries.astype(jnp.float32).reshape(seq_count, KVH, group, HD)
    key_f = cached_keys.astype(jnp.float32).reshape(seq_count, POS, KVH, HD)
    value_f = cached_values.astype(jnp.float32).reshape(seq_count, POS, KVH, HD)
    scores = jnp.einsum('skqd,spkd->skqp', query_f, key_f, precision=lax.Precision.HIGHEST) / math.sqrt(HD)
    in_cache = (jnp.arange(POS, dtype=jnp.int32)[None, :] < lengths[:, None])[:, None, None, :]
    masked = jnp.where(in_cache, scores, jnp.float32(-1e+30))
    row_top = lax.optimization_barrier(jnp.max(masked, axis=-1, keepdims=True))
    weights = jnp.exp(masked - row_top).astype(jnp.bfloat16)
    weight_total = lax.optimization_barrier(jnp.sum(weights.astype(jnp.float32), axis=-1))
    summed = jnp.einsum('skqp,spkd->skqd', weights.astype(jnp.float32), value_f, precision=lax.Precision.HIGHEST)
    return (summed / weight_total[..., None]).reshape(seq_count, QH * HD).astype(jnp.bfloat16)

def mixture(tokens, routes, gate_values, expert_in, expert_out):
    tok_total = tokens.shape[0]
    row_limit = tok_total // TOK_DEV * CAP
    token_ids = jnp.arange(tok_total, dtype=jnp.int32)
    gate_float = gate_values.astype(jnp.float32)

    def per_expert(carry, expert_id):
        chosen = routes == expert_id
        member = jnp.any(chosen, axis=1)
        gate_here = lax.optimization_barrier(jnp.sum(jnp.where(chosen, gate_float, jnp.float32(0.0)), axis=1))
        order = jnp.cumsum(member.astype(jnp.int32)) - 1
        target = jnp.where(member, order, row_limit).astype(jnp.int32)
        picked = jnp.zeros((row_limit,), jnp.int32).at[target].set(token_ids, mode='drop')
        weight_here = jnp.zeros((row_limit,), jnp.float32).at[target].set(gate_here, mode='drop')
        slot_rows = tokens[picked]
        hidden = jax.nn.silu(jnp.dot(slot_rows, expert_in[expert_id], preferred_element_type=jnp.float32)).astype(jnp.bfloat16)
        produced = jnp.dot(hidden, expert_out[expert_id], preferred_element_type=jnp.float32).astype(jnp.bfloat16)
        carry = carry.at[picked].add(weight_here[:, None] * produced.astype(jnp.float32))
        return (carry, None)
    start_sum = jnp.zeros(tokens.shape, jnp.float32)
    final_sum, unused = lax.scan(per_expert, start_sum, jnp.arange(EXPERTS, dtype=jnp.int32))
    return final_sum.astype(jnp.bfloat16)

def reference(tokens, routes, gate_values, expert_in, expert_out, queries, cached_keys, cached_values, lengths):
    moe_out = mixture(tokens, routes, gate_values, expert_in, expert_out)
    attention_out = attend(queries, cached_keys, cached_values, lengths)
    return (moe_out, attention_out)
```

```python
import functools
import math

import jax
import jax.numpy as jnp
from jax import lax
from jax.experimental import pallas as pl
from jax.experimental.pallas import tpu as pltpu
from jax.sharding import PartitionSpec as P

KVH = 4
HD = 128


def attend_local(queries, cached_keys, cached_values, lengths):
    seq_count = queries.shape[0]
    half_span = cached_keys.shape[1]
    group = queries.shape[1] // (KVH * HD)
    first_pos = lax.axis_index("cuts") * half_span
    positions = first_pos + jnp.arange(half_span, dtype=jnp.int32)
    in_cache = (positions[None, :] < lengths[:, None])[:, None, None, :]
    query_blocks = queries.reshape(seq_count, KVH, group, HD)
    key_blocks = cached_keys.reshape(seq_count, half_span, KVH, HD)
    value_blocks = cached_values.reshape(seq_count, half_span, KVH, HD)
    scores = jnp.einsum(
        "skqd,spkd->skqp", query_blocks, key_blocks, preferred_element_type=jnp.float32
    ) / math.sqrt(HD)
    masked = jnp.where(in_cache, scores, jnp.float32(-1e30))
    local_top = jnp.max(masked, axis=-1)
    row_top = lax.pmax(local_top, "cuts")
    weights = jnp.exp(masked - row_top[..., None]).astype(jnp.bfloat16)
    weight_total = jnp.sum(weights.astype(jnp.float32), axis=-1)
    summed = jnp.einsum(
        "skqp,spkd->skqd", weights, value_blocks, preferred_element_type=jnp.float32
    )
    weight_total, summed = lax.psum((weight_total, summed), "cuts")
    return (
        (summed / weight_total[..., None]).reshape(seq_count, KVH * group * HD).astype(jnp.bfloat16)
    )


def route_experts(tokens, routes, gate_values, expert_in, expert_out):
    tok_rows, width = tokens.shape
    top_count = routes.shape[1]
    experts_here = lax.axis_size("expert")
    capacity = min(tok_rows, 2 * tok_rows * top_count // experts_here)
    expert_ids = jnp.arange(experts_here, dtype=jnp.int32)
    chosen = routes[:, :, None] == expert_ids[None, None, :]
    member = jnp.sum(chosen, axis=1).astype(jnp.float32)
    gate_here = jnp.sum(
        jnp.where(chosen, gate_values.astype(jnp.float32)[:, :, None], jnp.float32(0.0)), axis=1
    )
    earlier = (jnp.arange(tok_rows)[:, None] > jnp.arange(tok_rows)[None, :]).astype(jnp.float32)
    slot_index = jnp.dot(earlier, member, precision=lax.Precision.HIGHEST)
    placed = (slot_index[:, :, None] == jnp.arange(capacity, dtype=jnp.float32)[None, None, :]) & (
        member[:, :, None] > 0.5
    )
    send_matrix = placed.astype(jnp.bfloat16).reshape(tok_rows, experts_here * capacity)
    combine_matrix = (
        (placed.astype(jnp.float32) * gate_here[:, :, None])
        .astype(jnp.bfloat16)
        .reshape(tok_rows, experts_here * capacity)
    )
    outgoing = jnp.einsum("tr,td->rd", send_matrix, tokens, preferred_element_type=jnp.float32)
    outgoing = outgoing.astype(jnp.bfloat16).reshape(experts_here, capacity, width)
    arrived = lax.all_to_all(outgoing, "expert", split_axis=0, concat_axis=0, tiled=True)
    slot_rows = arrived.reshape(-1, width)
    hidden = jax.nn.silu(
        jnp.dot(
            lax.all_gather(slot_rows, "cuts", axis=0, tiled=True),
            expert_in[0],
            preferred_element_type=jnp.float32,
        )
    ).astype(jnp.bfloat16)
    produced = lax.psum_scatter(
        jnp.dot(hidden, expert_out[0], preferred_element_type=jnp.float32),
        "cuts",
        scatter_dimension=0,
        tiled=True,
    ).astype(jnp.bfloat16)
    returned = lax.all_to_all(
        produced.reshape(arrived.shape), "expert", split_axis=0, concat_axis=0, tiled=True
    )
    combined = jnp.dot(
        combine_matrix,
        returned.reshape(experts_here * capacity, width),
        preferred_element_type=jnp.float32,
    )
    return combined.astype(jnp.bfloat16)


LANES = 128
VMEM = pl.BlockSpec(memory_space=pltpu.VMEM)
SMEM = pl.BlockSpec(memory_space=pltpu.SMEM)


def attend_kernel(lengths_ref, query_ref, key_ref, value_ref, out_ref):
    head_count = query_ref.shape[0]
    span = key_ref.shape[0]
    group = head_count // KVH
    live = lax.broadcasted_iota(jnp.int32, (group, span), 1) < lengths_ref[0]
    for k in range(KVH):
        rows = slice(k * group, (k + 1) * group)
        columns = slice(k * HD, (k + 1) * HD)
        scores = lax.dot_general(
            query_ref[rows, :],
            key_ref[:, columns],
            (((1,), (1,)), ((), ())),
            preferred_element_type=jnp.float32,
        ) * (1.0 / math.sqrt(HD))
        masked = jnp.where(live, scores, jnp.float32(-1e30))
        top = jnp.max(masked, axis=1, keepdims=True)
        weights = jnp.exp(masked - top).astype(jnp.bfloat16)
        total = jnp.sum(weights.astype(jnp.float32), axis=1, keepdims=True)
        summed = jnp.dot(weights, value_ref[:, columns], preferred_element_type=jnp.float32)
        out_ref[rows, :] = (summed / total).astype(out_ref.dtype)


def attend_whole(queries, cached_keys, cached_values, lengths):
    seq_count, width = queries.shape
    head_count = width // HD
    span = cached_keys.shape[1]
    outs = []
    for s in range(seq_count):
        outs.append(
            pl.pallas_call(
                attend_kernel,
                out_shape=jax.ShapeDtypeStruct((head_count, HD), jnp.bfloat16),
                in_specs=[SMEM, VMEM, VMEM, VMEM],
                out_specs=VMEM,
                compiler_params=pltpu.CompilerParams(vmem_limit_bytes=16 << 20),
                cost_estimate=pl.CostEstimate(
                    flops=4 * head_count * HD * span,
                    bytes_accessed=4 * span * KVH * HD,
                    transcendentals=head_count * span,
                ),
                name="attention",
            )(
                lengths[s : s + 1],
                queries[s].reshape(head_count, HD),
                cached_keys[s],
                cached_values[s],
            ).reshape(1, width)
        )
    return jnp.concatenate(outs, axis=0) if seq_count > 1 else outs[0]


def expert_kernel(expert_ref, rows_ref, in_ref, out_proj_ref, result_ref):
    width = in_ref.shape[0]
    gates = rows_ref[:, width:].astype(jnp.float32)
    lane = lax.broadcasted_iota(jnp.int32, gates.shape, 1)
    gate = jnp.sum(jnp.where(lane == expert_ref[0], gates, 0.0), axis=1, keepdims=True)
    pre = jnp.dot(rows_ref[:, :width], in_ref[...], preferred_element_type=jnp.float32)
    hidden = (pre / (1.0 + jnp.exp(-pre))).astype(jnp.bfloat16)
    produced = jnp.dot(hidden, out_proj_ref[...], preferred_element_type=jnp.float32)
    result_ref[...] = (produced * gate).astype(result_ref.dtype)


def run_expert(expert, rows, expert_in, expert_out, kind):
    count = rows.shape[0]
    width, units = expert_in.shape
    return pl.pallas_call(
        expert_kernel,
        out_shape=jax.ShapeDtypeStruct((count, width), kind),
        in_specs=[SMEM, VMEM, VMEM, VMEM],
        out_specs=VMEM,
        compiler_params=pltpu.CompilerParams(vmem_limit_bytes=24 << 20),
        cost_estimate=pl.CostEstimate(
            flops=4 * count * width * units,
            bytes_accessed=6 * count * width,
            transcendentals=count * units,
        ),
        name="expert",
    )(expert, rows, expert_in, expert_out)


def swap(block, distance):
    count = lax.axis_size("expert")
    return lax.ppermute(block, "expert", [(i, i ^ distance) for i in range(count)])


def route_spread(tokens, routes, gate_values, expert_in, expert_out):
    tok_rows, width = tokens.shape
    experts_here = lax.axis_size("expert")
    far = [8 * k for k in range(1, experts_here // 8)]
    near = [2, 4, 6]
    wide = jnp.float32
    lanes = jnp.arange(-(-experts_here // LANES) * LANES, dtype=jnp.int32)
    chosen = routes[:, :, None] == lanes[None, None, :]
    gates = jnp.sum(jnp.where(chosen, gate_values[:, :, None].astype(wide), 0.0), axis=1)
    own = jnp.concatenate([tokens, gates.astype(jnp.bfloat16)], axis=1)
    expert = lax.axis_index("expert").astype(jnp.int32).reshape(1)

    column = jnp.concatenate([own] + [swap(own, d) for d in far], axis=0)
    size = column.shape[0]
    arrived = [column] + [swap(column, d) for d in near]
    partial = []
    for first in (0, 2):
        rows = jnp.concatenate(arrived[first : first + 2], axis=0)
        other = swap(rows, 1)
        kept = run_expert(expert, rows, expert_in[0], expert_out[0], wide)
        sent = run_expert(expert, other, expert_in[0], expert_out[0], jnp.bfloat16)
        back = swap(sent, 1)
        total = kept + back.astype(wide)
        partial += [total[:size], total[size:]]
    total = partial[0]
    for block, d in zip(partial[1:], near):
        total = total + swap(block.astype(jnp.bfloat16), d).astype(wide)
    final = total[:tok_rows]
    for i, d in enumerate(far):
        block = total[(i + 1) * tok_rows : (i + 2) * tok_rows].astype(jnp.bfloat16)
        final = final + swap(block, d).astype(wide)
    return final.astype(jnp.bfloat16)


def on_device(
    spread,
    tokens,
    routes,
    gate_values,
    expert_in,
    expert_out,
    queries,
    cached_keys,
    cached_values,
    lengths,
):
    whole_cache = lax.axis_size("cuts") == 1
    attend = attend_whole if whole_cache else attend_local
    attention_out = attend(queries, cached_keys, cached_values, lengths)
    route = route_spread if spread else route_experts
    moe_out = route(tokens, routes, gate_values, expert_in, expert_out)
    return (moe_out, attention_out)


def solution(mesh):
    sizes = dict(mesh.shape)
    spread = sizes["cuts"] == 1 and sizes["expert"] in (8, 16, 32)
    in_specs = (
        P(("groups", "expert", "cuts"), None),
        P(("groups", "expert", "cuts"), None),
        P(("groups", "expert", "cuts"), None),
        P("expert", None, "cuts"),
        P("expert", "cuts", None),
        P(("groups", "expert"), None),
        P(("groups", "expert"), "cuts", None),
        P(("groups", "expert"), "cuts", None),
        P(("groups", "expert")),
    )
    out_specs = (P(("groups", "expert", "cuts"), None), P(("groups", "expert"), None))
    return jax.shard_map(
        functools.partial(on_device, spread),
        mesh=mesh,
        in_specs=in_specs,
        out_specs=out_specs,
        check_vma=False,
    )
```

```python
import functools
import math

import jax
import jax.numpy as jnp
from jax import lax
from jax.experimental import pallas as pl
from jax.experimental.pallas import tpu as pltpu
from jax.sharding import PartitionSpec as P

KVH = 4
HD = 128


def attend_local(queries, cached_keys, cached_values, lengths):
    seq_count = queries.shape[0]
    half_span = cached_keys.shape[1]
    group = queries.shape[1] // (KVH * HD)
    first_pos = lax.axis_index("cuts") * half_span
    positions = first_pos + jnp.arange(half_span, dtype=jnp.int32)
    in_cache = (positions[None, :] < lengths[:, None])[:, None, None, :]
    query_blocks = queries.reshape(seq_count, KVH, group, HD)
    key_blocks = cached_keys.reshape(seq_count, half_span, KVH, HD)
    value_blocks = cached_values.reshape(seq_count, half_span, KVH, HD)
    scores = jnp.einsum(
        "skqd,spkd->skqp", query_blocks, key_blocks, preferred_element_type=jnp.float32
    ) / math.sqrt(HD)
    masked = jnp.where(in_cache, scores, jnp.float32(-1e30))
    local_top = jnp.max(masked, axis=-1)
    row_top = lax.pmax(local_top, "cuts")
    weights = jnp.exp(masked - row_top[..., None]).astype(jnp.bfloat16)
    weight_total = jnp.sum(weights.astype(jnp.float32), axis=-1)
    summed = jnp.einsum(
        "skqp,spkd->skqd", weights, value_blocks, preferred_element_type=jnp.float32
    )
    weight_total, summed = lax.psum((weight_total, summed), "cuts")
    return (
        (summed / weight_total[..., None]).reshape(seq_count, KVH * group * HD).astype(jnp.bfloat16)
    )


def route_experts(tokens, routes, gate_values, expert_in, expert_out):
    tok_rows, width = tokens.shape
    top_count = routes.shape[1]
    experts_here = lax.axis_size("expert")
    capacity = min(tok_rows, 2 * tok_rows * top_count // experts_here)
    expert_ids = jnp.arange(experts_here, dtype=jnp.int32)
    chosen = routes[:, :, None] == expert_ids[None, None, :]
    member = jnp.sum(chosen, axis=1).astype(jnp.float32)
    gate_here = jnp.sum(
        jnp.where(chosen, gate_values.astype(jnp.float32)[:, :, None], jnp.float32(0.0)), axis=1
    )
    earlier = (jnp.arange(tok_rows)[:, None] > jnp.arange(tok_rows)[None, :]).astype(jnp.float32)
    slot_index = jnp.dot(earlier, member, precision=lax.Precision.HIGHEST)
    placed = (slot_index[:, :, None] == jnp.arange(capacity, dtype=jnp.float32)[None, None, :]) & (
        member[:, :, None] > 0.5
    )
    send_matrix = placed.astype(jnp.bfloat16).reshape(tok_rows, experts_here * capacity)
    combine_matrix = (
        (placed.astype(jnp.float32) * gate_here[:, :, None])
        .astype(jnp.bfloat16)
        .reshape(tok_rows, experts_here * capacity)
    )
    outgoing = jnp.einsum("tr,td->rd", send_matrix, tokens, preferred_element_type=jnp.float32)
    outgoing = outgoing.astype(jnp.bfloat16).reshape(experts_here, capacity, width)
    arrived = lax.all_to_all(outgoing, "expert", split_axis=0, concat_axis=0, tiled=True)
    slot_rows = arrived.reshape(-1, width)
    hidden = jax.nn.silu(
        jnp.dot(
            lax.all_gather(slot_rows, "cuts", axis=0, tiled=True),
            expert_in[0],
            preferred_element_type=jnp.float32,
        )
    ).astype(jnp.bfloat16)
    produced = lax.psum_scatter(
        jnp.dot(hidden, expert_out[0], preferred_element_type=jnp.float32),
        "cuts",
        scatter_dimension=0,
        tiled=True,
    ).astype(jnp.bfloat16)
    returned = lax.all_to_all(
        produced.reshape(arrived.shape), "expert", split_axis=0, concat_axis=0, tiled=True
    )
    combined = jnp.dot(
        combine_matrix,
        returned.reshape(experts_here * capacity, width),
        preferred_element_type=jnp.float32,
    )
    return combined.astype(jnp.bfloat16)


LANES = 128
VMEM = pl.BlockSpec(memory_space=pltpu.VMEM)
SMEM = pl.BlockSpec(memory_space=pltpu.SMEM)
ANYWHERE = pl.BlockSpec(memory_space=pl.ANY)
HBM = pl.BlockSpec(memory_space=pltpu.HBM)


def far_off(x):
    return pltpu.with_memory_space_constraint(x, pltpu.HBM)


def label_kernel(tokens_hbm, routes_hbm, gates_hbm, own_ref, routes_ref, gates_ref, sems):
    tok_rows, width = tokens_hbm.shape
    lanes = own_ref.shape[1] - width
    copies = [
        pltpu.make_async_copy(tokens_hbm, own_ref.at[:, pl.ds(0, width)], sems.at[0]),
        pltpu.make_async_copy(routes_hbm, routes_ref, sems.at[1]),
        pltpu.make_async_copy(gates_hbm, gates_ref, sems.at[2]),
    ]
    for copy in copies:
        copy.start()
    copies[1].wait()
    copies[2].wait()
    routes = routes_ref[...]
    gates = gates_ref[...].astype(jnp.float32)
    ids = lax.broadcasted_iota(jnp.int32, (lanes, tok_rows), 0)
    spread = jnp.zeros((lanes, tok_rows), jnp.float32)
    for k in range(routes.shape[0]):
        spread += jnp.where(ids == routes[k : k + 1, :], gates[k : k + 1, :], 0.0)
    places = (tok_rows, tok_rows)
    same = lax.broadcasted_iota(jnp.int32, places, 0) == lax.broadcasted_iota(jnp.int32, places, 1)
    turned = lax.dot_general(
        same.astype(jnp.bfloat16),
        spread.astype(jnp.bfloat16),
        (((1,), (1,)), ((), ())),
        preferred_element_type=jnp.float32,
    )
    own_ref[:, width:] = turned.astype(own_ref.dtype)
    copies[0].wait()


def label_tokens(tokens, routes, gate_values, experts):
    tok_rows, width = tokens.shape
    lanes = -(-experts // LANES) * LANES
    return pl.pallas_call(
        label_kernel,
        out_shape=jax.ShapeDtypeStruct((tok_rows, width + lanes), jnp.bfloat16),
        in_specs=[HBM] * 3,
        out_specs=VMEM,
        scratch_shapes=[
            pltpu.VMEM(routes.shape[::-1], routes.dtype),
            pltpu.VMEM(gate_values.shape[::-1], gate_values.dtype),
            pltpu.SemaphoreType.DMA((3,)),
        ],
        compiler_params=pltpu.CompilerParams(vmem_limit_bytes=4 << 20),
        name="label",
    )(far_off(tokens), far_off(routes.T), far_off(gate_values.T))


def attend_kernel(
    lengths_ref, query_ref, key_hbm, value_hbm, in_hbm, proj_hbm, out_ref, in_ref, proj_ref,
    key_ref, value_ref, sems
):
    pairs = ((key_hbm, key_ref), (value_hbm, value_ref), (in_hbm, in_ref), (proj_hbm, proj_ref))
    copies = [pltpu.make_async_copy(a, b, sems.at[i]) for i, (a, b) in enumerate(pairs)]
    for copy in copies:
        copy.start()
    head_count = query_ref.shape[1] // HD
    span = key_ref.shape[0]
    group = head_count // KVH
    query = query_ref[...].astype(jnp.float32)
    heads = [query[:, i * HD : (i + 1) * HD] for i in range(head_count)]
    live = lax.broadcasted_iota(jnp.int32, (group, span), 1) < lengths_ref[0]
    copies[0].wait()
    for k in range(KVH):
        rows = slice(k * group, (k + 1) * group)
        columns = slice(k * HD, (k + 1) * HD)
        scores = lax.dot_general(
            jnp.concatenate(heads[rows], axis=0).astype(jnp.bfloat16),
            key_ref[:, columns],
            (((1,), (1,)), ((), ())),
            preferred_element_type=jnp.float32,
        ) * (1.0 / math.sqrt(HD))
        masked = jnp.where(live, scores, jnp.float32(-1e30))
        top = jnp.max(masked, axis=1, keepdims=True)
        weights = jnp.exp(masked - top).astype(jnp.bfloat16)
        total = jnp.sum(weights.astype(jnp.float32), axis=1, keepdims=True)
        if k == 0:
            copies[1].wait()
        summed = jnp.dot(weights, value_ref[:, columns], preferred_element_type=jnp.float32)
        out_ref[rows, :] = (summed / total).astype(out_ref.dtype)
    copies[2].wait()
    copies[3].wait()


def attend_and_fetch(queries, cached_keys, cached_values, lengths, expert_in, expert_out):
    width = queries.shape[1]
    head_count = width // HD
    span = cached_keys.shape[1]
    attended, near_in, near_out = pl.pallas_call(
        attend_kernel,
        out_shape=[
            jax.ShapeDtypeStruct((head_count, HD), jnp.bfloat16),
            pltpu.VMEM(expert_in.shape[1:], jnp.bfloat16),
            pltpu.VMEM(expert_out.shape[1:], jnp.bfloat16),
        ],
        in_specs=[SMEM, VMEM] + [HBM] * 4,
        out_specs=[VMEM] * 3,
        scratch_shapes=[
            pltpu.VMEM(cached_keys.shape[1:], jnp.bfloat16),
            pltpu.VMEM(cached_values.shape[1:], jnp.bfloat16),
            pltpu.SemaphoreType.DMA((4,)),
        ],
        compiler_params=pltpu.CompilerParams(vmem_limit_bytes=14 << 20),
        cost_estimate=pl.CostEstimate(
            flops=4 * head_count * HD * span,
            bytes_accessed=4 * span * KVH * HD + 4 * expert_in.size + 4 * expert_out.size,
            transcendentals=head_count * span,
        ),
        name="attention",
    )(
        lengths,
        queries,
        *(far_off(a[0]) for a in (cached_keys, cached_values, expert_in, expert_out)),
    )
    return attended, near_in, near_out


def stack_kernel(*refs):
    parts, out_ref = refs[:-2], refs[-1]
    size = parts[0].shape[0]
    for i, part in enumerate(parts):
        out_ref[i * size : (i + 1) * size, :] = part[...]


def stack_rows(parts, after):
    size, width = parts[0].shape
    return pl.pallas_call(
        stack_kernel,
        out_shape=jax.ShapeDtypeStruct((size * len(parts), width), parts[0].dtype),
        in_specs=[VMEM] * len(parts) + [ANYWHERE],
        out_specs=VMEM,
        compiler_params=pltpu.CompilerParams(vmem_limit_bytes=4 << 20),
        name="stack",
    )(*parts, after)


def expert_kernel(part_count, *refs):
    parts, (in_ref, proj_ref), results = (
        refs[:part_count], refs[part_count : part_count + 2], refs[part_count + 2 :]
    )
    width = in_ref.shape[0]
    rows = jnp.concatenate([part[:, :width] for part in parts], axis=0)
    gates = jnp.concatenate([part[:, width:] for part in parts], axis=0).astype(jnp.float32)
    lane = lax.broadcasted_iota(jnp.int32, gates.shape, 1)
    gate = jnp.sum(jnp.where(lane == lax.axis_index("expert"), gates, 0.0), axis=1, keepdims=True)
    pre = jnp.dot(rows, in_ref[...], preferred_element_type=jnp.float32)
    hidden = (pre / (1.0 + jnp.exp(-pre))).astype(jnp.bfloat16)
    produced = jnp.dot(hidden, proj_ref[...], preferred_element_type=jnp.float32) * gate
    first = 0
    for result in results:
        size = result.shape[0]
        result[...] = produced[first : first + size].astype(result.dtype)
        first += size


def run_expert(parts, near_in, near_out, results):
    count = sum(part.shape[0] for part in parts)
    width, units = near_in.shape
    return pl.pallas_call(
        functools.partial(expert_kernel, len(parts)),
        out_shape=[jax.ShapeDtypeStruct((size, width), kind) for size, kind in results],
        in_specs=[VMEM] * (len(parts) + 2),
        out_specs=[VMEM] * len(results),
        compiler_params=pltpu.CompilerParams(vmem_limit_bytes=14 << 20),
        cost_estimate=pl.CostEstimate(
            flops=4 * count * width * units,
            bytes_accessed=6 * count * width,
            transcendentals=count * units,
        ),
        name="expert",
    )(*parts, hold(near_in), hold(near_out))


def hold(x):
    return pltpu.with_memory_space_constraint(x, pltpu.VMEM)


def swap(block, distance):
    count = lax.axis_size("expert")
    return lax.ppermute(block, "expert", [(i, i ^ distance) for i in range(count)])


def spread_step(
    tokens, routes, gate_values, expert_in, expert_out, queries, cached_keys, cached_values, lengths
):
    tok_rows = tokens.shape[0]
    experts_here = lax.axis_size("expert")
    far = [8 * k for k in range(1, experts_here // 8)]
    wide, half = jnp.float32, jnp.bfloat16
    own = label_tokens(tokens, routes, gate_values, experts_here)
    arrived = [swap(own, d) for d in far]
    attended, near_in, near_out = attend_and_fetch(
        queries, cached_keys, cached_values, lengths, expert_in, expert_out
    )
    column = stack_rows([own] + arrived, attended)
    size = column.shape[0]
    mid = size // 2

    def gated(parts, results):
        return run_expert(parts, near_in, near_out, results)

    by_x, by_y = swap(column, 2), swap(column, 4)
    pair = swap(column, 1)
    kept_own, sent_own = gated([column, pair], [(size, wide), (size, half)])
    back_own = swap(sent_own, 1)
    corner = [swap(by_y[:mid], 2), swap(by_x[mid:], 4)]
    pair_x, pair_y = swap(by_x, 1), swap(by_y, 1)
    kept_x, kept_y = gated([by_x, by_y], [(size, wide)] * 2)
    sent_x, sent_y = gated([pair_x, pair_y], [(size, half)] * 2)
    back_x, back_y = swap(sent_x, 1), swap(sent_y, 1)
    pair_corner = [swap(part, 1) for part in corner]
    kept_corner, sent_corner = gated(corner + pair_corner, [(size, wide), (size, half)])
    back_corner = swap(sent_corner, 1)

    total = kept_own + back_own.astype(wide)
    for kept, back, d in ((kept_x, back_x, 2), (kept_y, back_y, 4), (kept_corner, back_corner, 6)):
        total = total + swap((kept + back.astype(wide)).astype(half), d).astype(wide)
    final = total[:tok_rows]
    for i, d in enumerate(far):
        block = total[(i + 1) * tok_rows : (i + 2) * tok_rows].astype(half)
        final = final + swap(block, d).astype(wide)
    return final.astype(half), attended.reshape(queries.shape)


def on_device(
    tokens, routes, gate_values, expert_in, expert_out, queries, cached_keys, cached_values, lengths
):
    moe_out = route_experts(tokens, routes, gate_values, expert_in, expert_out)
    attention_out = attend_local(queries, cached_keys, cached_values, lengths)
    return (moe_out, attention_out)


def solution(mesh):
    sizes = dict(mesh.shape)
    spread = sizes["cuts"] == 1 and sizes["expert"] in (8, 16, 32)
    in_specs = (
        P(("groups", "expert", "cuts"), None),
        P(("groups", "expert", "cuts"), None),
        P(("groups", "expert", "cuts"), None),
        P("expert", None, "cuts"),
        P("expert", "cuts", None),
        P(("groups", "expert"), None),
        P(("groups", "expert"), "cuts", None),
        P(("groups", "expert"), "cuts", None),
        P(("groups", "expert")),
    )
    out_specs = (P(("groups", "expert", "cuts"), None), P(("groups", "expert"), None))
    return jax.shard_map(
        spread_step if spread else on_device,
        mesh=mesh,
        in_specs=in_specs,
        out_specs=out_specs,
        check_vma=False,
    )
```

```python
import functools
import math

import jax
import jax.numpy as jnp
from jax import lax
from jax.experimental import pallas as pl
from jax.experimental.pallas import tpu as pltpu
from jax.sharding import PartitionSpec as P

KVH = 4
HD = 128


def attend_local(queries, cached_keys, cached_values, lengths):
    seq_count = queries.shape[0]
    half_span = cached_keys.shape[1]
    group = queries.shape[1] // (KVH * HD)
    first_pos = lax.axis_index("cuts") * half_span
    positions = first_pos + jnp.arange(half_span, dtype=jnp.int32)
    in_cache = (positions[None, :] < lengths[:, None])[:, None, None, :]
    query_blocks = queries.reshape(seq_count, KVH, group, HD)
    key_blocks = cached_keys.reshape(seq_count, half_span, KVH, HD)
    value_blocks = cached_values.reshape(seq_count, half_span, KVH, HD)
    scores = jnp.einsum(
        "skqd,spkd->skqp", query_blocks, key_blocks, preferred_element_type=jnp.float32
    ) / math.sqrt(HD)
    masked = jnp.where(in_cache, scores, jnp.float32(-1e30))
    local_top = jnp.max(masked, axis=-1)
    row_top = lax.pmax(local_top, "cuts")
    weights = jnp.exp(masked - row_top[..., None]).astype(jnp.bfloat16)
    weight_total = jnp.sum(weights.astype(jnp.float32), axis=-1)
    summed = jnp.einsum(
        "skqp,spkd->skqd", weights, value_blocks, preferred_element_type=jnp.float32
    )
    weight_total, summed = lax.psum((weight_total, summed), "cuts")
    return (
        (summed / weight_total[..., None]).reshape(seq_count, KVH * group * HD).astype(jnp.bfloat16)
    )


def route_experts(tokens, routes, gate_values, expert_in, expert_out):
    tok_rows, width = tokens.shape
    top_count = routes.shape[1]
    experts_here = lax.axis_size("expert")
    capacity = min(tok_rows, 2 * tok_rows * top_count // experts_here)
    expert_ids = jnp.arange(experts_here, dtype=jnp.int32)
    chosen = routes[:, :, None] == expert_ids[None, None, :]
    member = jnp.sum(chosen, axis=1).astype(jnp.float32)
    gate_here = jnp.sum(
        jnp.where(chosen, gate_values.astype(jnp.float32)[:, :, None], jnp.float32(0.0)), axis=1
    )
    earlier = (jnp.arange(tok_rows)[:, None] > jnp.arange(tok_rows)[None, :]).astype(jnp.float32)
    slot_index = jnp.dot(earlier, member, precision=lax.Precision.HIGHEST)
    placed = (slot_index[:, :, None] == jnp.arange(capacity, dtype=jnp.float32)[None, None, :]) & (
        member[:, :, None] > 0.5
    )
    send_matrix = placed.astype(jnp.bfloat16).reshape(tok_rows, experts_here * capacity)
    combine_matrix = (
        (placed.astype(jnp.float32) * gate_here[:, :, None])
        .astype(jnp.bfloat16)
        .reshape(tok_rows, experts_here * capacity)
    )
    outgoing = jnp.einsum("tr,td->rd", send_matrix, tokens, preferred_element_type=jnp.float32)
    outgoing = outgoing.astype(jnp.bfloat16).reshape(experts_here, capacity, width)
    arrived = lax.all_to_all(outgoing, "expert", split_axis=0, concat_axis=0, tiled=True)
    slot_rows = arrived.reshape(-1, width)
    hidden = jax.nn.silu(
        jnp.dot(
            lax.all_gather(slot_rows, "cuts", axis=0, tiled=True),
            expert_in[0],
            preferred_element_type=jnp.float32,
        )
    ).astype(jnp.bfloat16)
    produced = lax.psum_scatter(
        jnp.dot(hidden, expert_out[0], preferred_element_type=jnp.float32),
        "cuts",
        scatter_dimension=0,
        tiled=True,
    ).astype(jnp.bfloat16)
    returned = lax.all_to_all(
        produced.reshape(arrived.shape), "expert", split_axis=0, concat_axis=0, tiled=True
    )
    combined = jnp.dot(
        combine_matrix,
        returned.reshape(experts_here * capacity, width),
        preferred_element_type=jnp.float32,
    )
    return combined.astype(jnp.bfloat16)


LANES = 128
VMEM = pl.BlockSpec(memory_space=pltpu.VMEM)
SMEM = pl.BlockSpec(memory_space=pltpu.SMEM)
ANYWHERE = pl.BlockSpec(memory_space=pl.ANY)
HBM = pl.BlockSpec(memory_space=pltpu.HBM)


def far_off(x):
    return pltpu.with_memory_space_constraint(x, pltpu.HBM)


def label_kernel(tokens_hbm, routes_hbm, gates_hbm, own_ref, routes_ref, gates_ref, sems):
    tok_rows, width = tokens_hbm.shape
    lanes = own_ref.shape[1] - width
    copies = [
        pltpu.make_async_copy(tokens_hbm, own_ref.at[:, pl.ds(0, width)], sems.at[0]),
        pltpu.make_async_copy(routes_hbm, routes_ref, sems.at[1]),
        pltpu.make_async_copy(gates_hbm, gates_ref, sems.at[2]),
    ]
    for copy in copies:
        copy.start()
    copies[1].wait()
    copies[2].wait()
    routes = routes_ref[...]
    gates = gates_ref[...].astype(jnp.float32)
    ids = lax.broadcasted_iota(jnp.int32, (lanes, tok_rows), 0)
    spread = jnp.zeros((lanes, tok_rows), jnp.float32)
    for k in range(routes.shape[0]):
        spread += jnp.where(ids == routes[k : k + 1, :], gates[k : k + 1, :], 0.0)
    places = (tok_rows, tok_rows)
    same = lax.broadcasted_iota(jnp.int32, places, 0) == lax.broadcasted_iota(jnp.int32, places, 1)
    turned = lax.dot_general(
        same.astype(jnp.bfloat16),
        spread.astype(jnp.bfloat16),
        (((1,), (1,)), ((), ())),
        preferred_element_type=jnp.float32,
    )
    own_ref[:, width:] = turned.astype(own_ref.dtype)
    copies[0].wait()


def label_tokens(tokens, routes, gate_values, experts):
    tok_rows, width = tokens.shape
    lanes = -(-experts // LANES) * LANES
    return pl.pallas_call(
        label_kernel,
        out_shape=jax.ShapeDtypeStruct((tok_rows, width + lanes), jnp.bfloat16),
        in_specs=[HBM] * 3,
        out_specs=VMEM,
        scratch_shapes=[
            pltpu.VMEM(routes.shape[::-1], routes.dtype),
            pltpu.VMEM(gate_values.shape[::-1], gate_values.dtype),
            pltpu.SemaphoreType.DMA((3,)),
        ],
        compiler_params=pltpu.CompilerParams(vmem_limit_bytes=4 << 20),
        name="label",
    )(far_off(tokens), far_off(routes.T), far_off(gate_values.T))


def attend_kernel(
    lengths_ref, query_ref, key_hbm, value_hbm, in_hbm, proj_hbm, out_ref, in_ref, proj_ref,
    key_ref, value_ref, sems
):
    pairs = ((key_hbm, key_ref), (value_hbm, value_ref), (in_hbm, in_ref), (proj_hbm, proj_ref))
    copies = [pltpu.make_async_copy(a, b, sems.at[i]) for i, (a, b) in enumerate(pairs)]
    for copy in copies:
        copy.start()
    head_count = query_ref.shape[1] // HD
    span = key_ref.shape[0]
    group = head_count // KVH
    query = query_ref[...].astype(jnp.float32)
    heads = [query[:, i * HD : (i + 1) * HD] for i in range(head_count)]
    live = lax.broadcasted_iota(jnp.int32, (group, span), 1) < lengths_ref[0]
    copies[0].wait()
    for k in range(KVH):
        rows = slice(k * group, (k + 1) * group)
        columns = slice(k * HD, (k + 1) * HD)
        scores = lax.dot_general(
            jnp.concatenate(heads[rows], axis=0).astype(jnp.bfloat16),
            key_ref[:, columns],
            (((1,), (1,)), ((), ())),
            preferred_element_type=jnp.float32,
        ) * (1.0 / math.sqrt(HD))
        masked = jnp.where(live, scores, jnp.float32(-1e30))
        top = jnp.max(masked, axis=1, keepdims=True)
        weights = jnp.exp(masked - top).astype(jnp.bfloat16)
        total = jnp.sum(weights.astype(jnp.float32), axis=1, keepdims=True)
        if k == 0:
            copies[1].wait()
        summed = jnp.dot(weights, value_ref[:, columns], preferred_element_type=jnp.float32)
        out_ref[rows, :] = (summed / total).astype(out_ref.dtype)
    copies[2].wait()
    copies[3].wait()


def attend_and_fetch(queries, cached_keys, cached_values, lengths, expert_in, expert_out):
    width = queries.shape[1]
    head_count = width // HD
    span = cached_keys.shape[1]
    attended, near_in, near_out = pl.pallas_call(
        attend_kernel,
        out_shape=[
            jax.ShapeDtypeStruct((head_count, HD), jnp.bfloat16),
            pltpu.VMEM(expert_in.shape[1:], jnp.bfloat16),
            pltpu.VMEM(expert_out.shape[1:], jnp.bfloat16),
        ],
        in_specs=[SMEM, VMEM] + [HBM] * 4,
        out_specs=[VMEM] * 3,
        scratch_shapes=[
            pltpu.VMEM(cached_keys.shape[1:], jnp.bfloat16),
            pltpu.VMEM(cached_values.shape[1:], jnp.bfloat16),
            pltpu.SemaphoreType.DMA((4,)),
        ],
        compiler_params=pltpu.CompilerParams(vmem_limit_bytes=14 << 20),
        cost_estimate=pl.CostEstimate(
            flops=4 * head_count * HD * span,
            bytes_accessed=4 * span * KVH * HD + 4 * expert_in.size + 4 * expert_out.size,
            transcendentals=head_count * span,
        ),
        name="attention",
    )(
        lengths,
        queries,
        *(far_off(a[0]) for a in (cached_keys, cached_values, expert_in, expert_out)),
    )
    return attended, near_in, near_out


def stack_kernel(part_count, *refs):
    parts, out_ref = refs[:part_count], refs[-1]
    size = parts[0].shape[0]
    for i, part in enumerate(parts):
        out_ref[i * size : (i + 1) * size, :] = part[...]


def stack_rows(parts, after=()):
    size, width = parts[0].shape
    return pl.pallas_call(
        functools.partial(stack_kernel, len(parts)),
        out_shape=jax.ShapeDtypeStruct((size * len(parts), width), parts[0].dtype),
        in_specs=[VMEM] * len(parts) + [ANYWHERE] * len(after),
        out_specs=VMEM,
        compiler_params=pltpu.CompilerParams(vmem_limit_bytes=4 << 20),
        name="stack",
    )(*parts, *after)


def expert_kernel(part_count, after_count, *refs):
    parts, (in_ref, proj_ref), results = (
        refs[:part_count], refs[part_count : part_count + 2], refs[part_count + 2 + after_count :]
    )
    width = in_ref.shape[0]
    rows = jnp.concatenate([part[:, :width] for part in parts], axis=0)
    gates = jnp.concatenate([part[:, width:] for part in parts], axis=0).astype(jnp.float32)
    lane = lax.broadcasted_iota(jnp.int32, gates.shape, 1)
    gate = jnp.sum(jnp.where(lane == lax.axis_index("expert"), gates, 0.0), axis=1, keepdims=True)
    pre = jnp.dot(rows, in_ref[...], preferred_element_type=jnp.float32)
    hidden = (pre / (1.0 + jnp.exp(-pre))).astype(jnp.bfloat16)
    produced = jnp.dot(hidden, proj_ref[...], preferred_element_type=jnp.float32) * gate
    first = 0
    for result in results:
        size = result.shape[0]
        result[...] = produced[first : first + size].astype(result.dtype)
        first += size


def run_expert(parts, near_in, near_out, results, after):
    count = sum(part.shape[0] for part in parts)
    width, units = near_in.shape
    return pl.pallas_call(
        functools.partial(expert_kernel, len(parts), len(after)),
        out_shape=[jax.ShapeDtypeStruct((size, width), kind) for size, kind in results],
        in_specs=[VMEM] * (len(parts) + 2) + [ANYWHERE] * len(after),
        out_specs=[VMEM] * len(results),
        compiler_params=pltpu.CompilerParams(vmem_limit_bytes=14 << 20),
        cost_estimate=pl.CostEstimate(
            flops=4 * count * width * units,
            bytes_accessed=6 * count * width,
            transcendentals=count * units,
        ),
        name="expert",
    )(*parts, hold(near_in), hold(near_out), *after)


def hold(x):
    return pltpu.with_memory_space_constraint(x, pltpu.VMEM)


def add_kernel(part_count, *refs):
    kept_ref, parts, result_ref = refs[0], refs[1 : part_count + 1], refs[-1]
    back = jnp.concatenate([part[...] for part in parts], axis=0).astype(jnp.float32)
    result_ref[...] = (kept_ref[...] + back).astype(result_ref.dtype)


def add_parts(kept, parts, after=()):
    return pl.pallas_call(
        functools.partial(add_kernel, len(parts)),
        out_shape=jax.ShapeDtypeStruct(kept.shape, parts[0].dtype),
        in_specs=[VMEM] * (len(parts) + 1) + [ANYWHERE] * len(after),
        out_specs=VMEM,
        compiler_params=pltpu.CompilerParams(vmem_limit_bytes=6 << 20),
        name="add",
    )(kept, *parts, *after)


def cut(block, count):
    rows = block.shape[0] // count
    return [block[i * rows : (i + 1) * rows] for i in range(count)]


def cross(block, even, odd):
    count = lax.axis_size("expert")
    pairs = [(i, i ^ (odd if i % 2 else even)) for i in range(count)]
    return lax.ppermute(block, "expert", pairs)


def swap(block, distance):
    count = lax.axis_size("expert")
    return lax.ppermute(block, "expert", [(i, i ^ distance) for i in range(count)])


def spread_step(
    tokens, routes, gate_values, expert_in, expert_out, queries, cached_keys, cached_values, lengths
):
    tok_rows = tokens.shape[0]
    experts_here = lax.axis_size("expert")
    far = [8 * k for k in range(1, experts_here // 8)]
    wide, half = jnp.float32, jnp.bfloat16
    own = label_tokens(tokens, routes, gate_values, experts_here)
    arrived = [swap(own, d) for d in far]
    attended, near_in, near_out = attend_and_fetch(
        queries, cached_keys, cached_values, lengths, expert_in, expert_out
    )

    def gated(parts, results, after=()):
        return run_expert(parts, near_in, near_out, results, after)

    column = stack_rows([own] + arrived, [attended])
    size = column.shape[0]
    mid = size // 2
    cuts_in, cuts_out = 2, 2
    split = [(size, wide)] + [(size // cuts_out, half)] * cuts_out

    def halves(block):
        return [swap(part, 1) for part in cut(block, cuts_in)]

    pair = swap(column, 1)
    side_a = cross(column, 2, 4)
    side_b = cross(pair, 2, 4)
    corner = cross(side_a, 5, 3)
    kept_a, *sent_a = gated([side_a] + halves(side_a), split)
    sum_a = add_parts(kept_a, [swap(part, 1) for part in sent_a])
    got_a = cross(sum_a, 2, 4)
    kept_b, *sent_b = gated([side_b] + halves(side_b), split, [sum_a])
    sum_b = add_parts(kept_b, [swap(part, 1) for part in sent_b])
    got_b = cross(sum_b, 2, 4)
    (kept_own, kept_pair) = gated([column, pair], [(size, wide)] * 2, [sum_b])
    kept_c, *sent_c = gated([corner] + halves(corner), split, [sum_b])
    sum_c = add_parts(kept_c, [swap(part, 1) for part in sent_c])
    got_c = swap(sum_c, 7)
    total = kept_own + got_a.astype(wide) + swap((kept_pair + got_b.astype(wide)).astype(half), 1).astype(wide)
    total = total + got_c.astype(wide)
    final = total[:tok_rows]
    for i, d in enumerate(far):
        block = total[(i + 1) * tok_rows : (i + 2) * tok_rows].astype(half)
        final = final + swap(block, d).astype(wide)
    return final.astype(half), attended.reshape(queries.shape)


def on_device(
    tokens, routes, gate_values, expert_in, expert_out, queries, cached_keys, cached_values, lengths
):
    moe_out = route_experts(tokens, routes, gate_values, expert_in, expert_out)
    attention_out = attend_local(queries, cached_keys, cached_values, lengths)
    return (moe_out, attention_out)


def solution(mesh):
    sizes = dict(mesh.shape)
    spread = sizes["cuts"] == 1 and sizes["expert"] in (8, 16, 32)
    in_specs = (
        P(("groups", "expert", "cuts"), None),
        P(("groups", "expert", "cuts"), None),
        P(("groups", "expert", "cuts"), None),
        P("expert", None, "cuts"),
        P("expert", "cuts", None),
        P(("groups", "expert"), None),
        P(("groups", "expert"), "cuts", None),
        P(("groups", "expert"), "cuts", None),
        P(("groups", "expert")),
    )
    out_specs = (P(("groups", "expert", "cuts"), None), P(("groups", "expert"), None))
    return jax.shard_map(
        spread_step if spread else on_device,
        mesh=mesh,
        in_specs=in_specs,
        out_specs=out_specs,
        check_vma=False,
    )
```

```python
import functools
import math

import jax
import jax.numpy as jnp
from jax import lax
from jax.experimental import pallas as pl
from jax.experimental.pallas import tpu as pltpu
from jax.sharding import PartitionSpec as P

KVH = 4
HD = 128


def attend_local(queries, cached_keys, cached_values, lengths):
    seq_count = queries.shape[0]
    half_span = cached_keys.shape[1]
    group = queries.shape[1] // (KVH * HD)
    first_pos = lax.axis_index("cuts") * half_span
    positions = first_pos + jnp.arange(half_span, dtype=jnp.int32)
    in_cache = (positions[None, :] < lengths[:, None])[:, None, None, :]
    query_blocks = queries.reshape(seq_count, KVH, group, HD)
    key_blocks = cached_keys.reshape(seq_count, half_span, KVH, HD)
    value_blocks = cached_values.reshape(seq_count, half_span, KVH, HD)
    scores = jnp.einsum(
        "skqd,spkd->skqp", query_blocks, key_blocks, preferred_element_type=jnp.float32
    ) / math.sqrt(HD)
    masked = jnp.where(in_cache, scores, jnp.float32(-1e30))
    local_top = jnp.max(masked, axis=-1)
    row_top = lax.pmax(local_top, "cuts")
    weights = jnp.exp(masked - row_top[..., None]).astype(jnp.bfloat16)
    weight_total = jnp.sum(weights.astype(jnp.float32), axis=-1)
    summed = jnp.einsum(
        "skqp,spkd->skqd", weights, value_blocks, preferred_element_type=jnp.float32
    )
    weight_total, summed = lax.psum((weight_total, summed), "cuts")
    return (
        (summed / weight_total[..., None]).reshape(seq_count, KVH * group * HD).astype(jnp.bfloat16)
    )


def route_experts(tokens, routes, gate_values, expert_in, expert_out):
    tok_rows, width = tokens.shape
    top_count = routes.shape[1]
    experts_here = lax.axis_size("expert")
    capacity = min(tok_rows, 2 * tok_rows * top_count // experts_here)
    expert_ids = jnp.arange(experts_here, dtype=jnp.int32)
    chosen = routes[:, :, None] == expert_ids[None, None, :]
    member = jnp.sum(chosen, axis=1).astype(jnp.float32)
    gate_here = jnp.sum(
        jnp.where(chosen, gate_values.astype(jnp.float32)[:, :, None], jnp.float32(0.0)), axis=1
    )
    earlier = (jnp.arange(tok_rows)[:, None] > jnp.arange(tok_rows)[None, :]).astype(jnp.float32)
    slot_index = jnp.dot(earlier, member, precision=lax.Precision.HIGHEST)
    placed = (slot_index[:, :, None] == jnp.arange(capacity, dtype=jnp.float32)[None, None, :]) & (
        member[:, :, None] > 0.5
    )
    send_matrix = placed.astype(jnp.bfloat16).reshape(tok_rows, experts_here * capacity)
    combine_matrix = (
        (placed.astype(jnp.float32) * gate_here[:, :, None])
        .astype(jnp.bfloat16)
        .reshape(tok_rows, experts_here * capacity)
    )
    outgoing = jnp.einsum("tr,td->rd", send_matrix, tokens, preferred_element_type=jnp.float32)
    outgoing = outgoing.astype(jnp.bfloat16).reshape(experts_here, capacity, width)
    arrived = lax.all_to_all(outgoing, "expert", split_axis=0, concat_axis=0, tiled=True)
    slot_rows = arrived.reshape(-1, width)
    hidden = jax.nn.silu(
        jnp.dot(
            lax.all_gather(slot_rows, "cuts", axis=0, tiled=True),
            expert_in[0],
            preferred_element_type=jnp.float32,
        )
    ).astype(jnp.bfloat16)
    produced = lax.psum_scatter(
        jnp.dot(hidden, expert_out[0], preferred_element_type=jnp.float32),
        "cuts",
        scatter_dimension=0,
        tiled=True,
    ).astype(jnp.bfloat16)
    returned = lax.all_to_all(
        produced.reshape(arrived.shape), "expert", split_axis=0, concat_axis=0, tiled=True
    )
    combined = jnp.dot(
        combine_matrix,
        returned.reshape(experts_here * capacity, width),
        preferred_element_type=jnp.float32,
    )
    return combined.astype(jnp.bfloat16)


LANES = 128
VMEM = pl.BlockSpec(memory_space=pltpu.VMEM)
SMEM = pl.BlockSpec(memory_space=pltpu.SMEM)
ANYWHERE = pl.BlockSpec(memory_space=pl.ANY)
HBM = pl.BlockSpec(memory_space=pltpu.HBM)


def far_off(x):
    return pltpu.with_memory_space_constraint(x, pltpu.HBM)


def label_kernel(tokens_hbm, routes_hbm, gates_hbm, own_ref, routes_ref, gates_ref, sems):
    tok_rows, width = tokens_hbm.shape
    lanes = own_ref.shape[1] - width
    copies = [
        pltpu.make_async_copy(tokens_hbm, own_ref.at[:, pl.ds(0, width)], sems.at[0]),
        pltpu.make_async_copy(routes_hbm, routes_ref, sems.at[1]),
        pltpu.make_async_copy(gates_hbm, gates_ref, sems.at[2]),
    ]
    for copy in copies:
        copy.start()
    copies[1].wait()
    copies[2].wait()
    routes = routes_ref[...]
    gates = gates_ref[...].astype(jnp.float32)
    ids = lax.broadcasted_iota(jnp.int32, (lanes, tok_rows), 0)
    spread = jnp.zeros((lanes, tok_rows), jnp.float32)
    for k in range(routes.shape[0]):
        spread += jnp.where(ids == routes[k : k + 1, :], gates[k : k + 1, :], 0.0)
    places = (tok_rows, tok_rows)
    same = lax.broadcasted_iota(jnp.int32, places, 0) == lax.broadcasted_iota(jnp.int32, places, 1)
    turned = lax.dot_general(
        same.astype(jnp.bfloat16),
        spread.astype(jnp.bfloat16),
        (((1,), (1,)), ((), ())),
        preferred_element_type=jnp.float32,
    )
    own_ref[:, width:] = turned.astype(own_ref.dtype)
    copies[0].wait()


def label_tokens(tokens, routes, gate_values, experts):
    tok_rows, width = tokens.shape
    lanes = -(-experts // LANES) * LANES
    return pl.pallas_call(
        label_kernel,
        out_shape=jax.ShapeDtypeStruct((tok_rows, width + lanes), jnp.bfloat16),
        in_specs=[HBM] * 3,
        out_specs=VMEM,
        scratch_shapes=[
            pltpu.VMEM(routes.shape[::-1], routes.dtype),
            pltpu.VMEM(gate_values.shape[::-1], gate_values.dtype),
            pltpu.SemaphoreType.DMA((3,)),
        ],
        compiler_params=pltpu.CompilerParams(vmem_limit_bytes=4 << 20),
        name="label",
    )(far_off(tokens), far_off(routes.T), far_off(gate_values.T))


def attend_kernel(
    lengths_ref, query_ref, key_hbm, value_hbm, in_hbm, proj_hbm, out_ref, in_ref, proj_ref,
    key_ref, value_ref, sems
):
    pairs = ((key_hbm, key_ref), (value_hbm, value_ref), (in_hbm, in_ref), (proj_hbm, proj_ref))
    copies = [pltpu.make_async_copy(a, b, sems.at[i]) for i, (a, b) in enumerate(pairs)]
    for copy in copies:
        copy.start()
    head_count = query_ref.shape[1] // HD
    span = key_ref.shape[0]
    group = head_count // KVH
    query = query_ref[...].astype(jnp.float32)
    heads = [query[:, i * HD : (i + 1) * HD] for i in range(head_count)]
    live = lax.broadcasted_iota(jnp.int32, (group, span), 1) < lengths_ref[0]
    copies[0].wait()
    for k in range(KVH):
        rows = slice(k * group, (k + 1) * group)
        columns = slice(k * HD, (k + 1) * HD)
        scores = lax.dot_general(
            jnp.concatenate(heads[rows], axis=0).astype(jnp.bfloat16),
            key_ref[:, columns],
            (((1,), (1,)), ((), ())),
            preferred_element_type=jnp.float32,
        ) * (1.0 / math.sqrt(HD))
        masked = jnp.where(live, scores, jnp.float32(-1e30))
        top = jnp.max(masked, axis=1, keepdims=True)
        weights = jnp.exp(masked - top).astype(jnp.bfloat16)
        total = jnp.sum(weights.astype(jnp.float32), axis=1, keepdims=True)
        if k == 0:
            copies[1].wait()
        summed = jnp.dot(weights, value_ref[:, columns], preferred_element_type=jnp.float32)
        out_ref[rows, :] = (summed / total).astype(out_ref.dtype)
    copies[2].wait()
    copies[3].wait()


def attend_and_fetch(queries, cached_keys, cached_values, lengths, expert_in, expert_out):
    width = queries.shape[1]
    head_count = width // HD
    span = cached_keys.shape[1]
    attended, near_in, near_out = pl.pallas_call(
        attend_kernel,
        out_shape=[
            jax.ShapeDtypeStruct((head_count, HD), jnp.bfloat16),
            pltpu.VMEM(expert_in.shape[1:], jnp.bfloat16),
            pltpu.VMEM(expert_out.shape[1:], jnp.bfloat16),
        ],
        in_specs=[SMEM, VMEM] + [HBM] * 4,
        out_specs=[VMEM] * 3,
        scratch_shapes=[
            pltpu.VMEM(cached_keys.shape[1:], jnp.bfloat16),
            pltpu.VMEM(cached_values.shape[1:], jnp.bfloat16),
            pltpu.SemaphoreType.DMA((4,)),
        ],
        compiler_params=pltpu.CompilerParams(vmem_limit_bytes=14 << 20),
        cost_estimate=pl.CostEstimate(
            flops=4 * head_count * HD * span,
            bytes_accessed=4 * span * KVH * HD + 4 * expert_in.size + 4 * expert_out.size,
            transcendentals=head_count * span,
        ),
        name="attention",
    )(
        lengths,
        queries,
        *(far_off(a[0]) for a in (cached_keys, cached_values, expert_in, expert_out)),
    )
    return attended, near_in, near_out


def stack_kernel(part_count, *refs):
    parts, out_ref = refs[:part_count], refs[-1]
    size = parts[0].shape[0]
    for i, part in enumerate(parts):
        out_ref[i * size : (i + 1) * size, :] = part[...]


def stack_rows(parts, after=()):
    size, width = parts[0].shape
    return pl.pallas_call(
        functools.partial(stack_kernel, len(parts)),
        out_shape=jax.ShapeDtypeStruct((size * len(parts), width), parts[0].dtype),
        in_specs=[VMEM] * len(parts) + [ANYWHERE] * len(after),
        out_specs=VMEM,
        compiler_params=pltpu.CompilerParams(vmem_limit_bytes=4 << 20),
        name="stack",
    )(*parts, *after)


def expert_kernel(part_count, after_count, *refs):
    parts, (in_ref, proj_ref), results = (
        refs[:part_count], refs[part_count : part_count + 2], refs[part_count + 2 + after_count :]
    )
    width = in_ref.shape[0]
    rows = jnp.concatenate([part[:, :width] for part in parts], axis=0)
    gates = jnp.concatenate([part[:, width:] for part in parts], axis=0).astype(jnp.float32)
    lane = lax.broadcasted_iota(jnp.int32, gates.shape, 1)
    gate = jnp.sum(jnp.where(lane == lax.axis_index("expert"), gates, 0.0), axis=1, keepdims=True)
    pre = jnp.dot(rows, in_ref[...], preferred_element_type=jnp.float32)
    hidden = (pre / (1.0 + jnp.exp(-pre))).astype(jnp.bfloat16)
    produced = jnp.dot(hidden, proj_ref[...], preferred_element_type=jnp.float32) * gate
    first = 0
    for result in results:
        size = result.shape[0]
        result[...] = produced[first : first + size].astype(result.dtype)
        first += size


def run_expert(parts, near_in, near_out, results, after):
    count = sum(part.shape[0] for part in parts)
    width, units = near_in.shape
    return pl.pallas_call(
        functools.partial(expert_kernel, len(parts), len(after)),
        out_shape=[jax.ShapeDtypeStruct((size, width), kind) for size, kind in results],
        in_specs=[VMEM] * (len(parts) + 2) + [ANYWHERE] * len(after),
        out_specs=[VMEM] * len(results),
        compiler_params=pltpu.CompilerParams(vmem_limit_bytes=14 << 20),
        cost_estimate=pl.CostEstimate(
            flops=4 * count * width * units,
            bytes_accessed=6 * count * width,
            transcendentals=count * units,
        ),
        name="expert",
    )(*parts, hold(near_in), hold(near_out), *after)


def hold(x):
    return pltpu.with_memory_space_constraint(x, pltpu.VMEM)


def add_kernel(part_count, *refs):
    kept_ref, parts, result_ref = refs[0], refs[1 : part_count + 1], refs[-1]
    back = jnp.concatenate([part[...] for part in parts], axis=0).astype(jnp.float32)
    result_ref[...] = (kept_ref[...] + back).astype(result_ref.dtype)


def add_parts(kept, parts, after=()):
    return pl.pallas_call(
        functools.partial(add_kernel, len(parts)),
        out_shape=jax.ShapeDtypeStruct(kept.shape, parts[0].dtype),
        in_specs=[VMEM] * (len(parts) + 1) + [ANYWHERE] * len(after),
        out_specs=VMEM,
        compiler_params=pltpu.CompilerParams(vmem_limit_bytes=6 << 20),
        name="add",
    )(kept, *parts, *after)


def finish_kernel(first, total_ref, block_ref, *part_refs):
    rows = part_refs[0].shape[0]
    for i, part_ref in enumerate(part_refs):
        at = slice(first + i * rows, first + (i + 1) * rows)
        block = block_ref[i * rows : (i + 1) * rows, :].astype(jnp.float32)
        part_ref[...] = (total_ref[at, :] + block).astype(part_ref.dtype)


def finish_rows(total, block, first, count):
    part = jax.ShapeDtypeStruct((block.shape[0] // count, block.shape[1]), block.dtype)
    return pl.pallas_call(
        functools.partial(finish_kernel, first),
        out_shape=[part] * count,
        in_specs=[VMEM] * 2,
        out_specs=[VMEM] * count,
        compiler_params=pltpu.CompilerParams(vmem_limit_bytes=4 << 20),
        name="finish",
    )(total, block)


def cut_kernel(count, block_ref, *refs):
    rows = block_ref.shape[0] // count
    for i, part_ref in enumerate(refs[-count:]):
        part_ref[...] = block_ref[i * rows : (i + 1) * rows, :]


def cut_rows(block, count, after=()):
    part = jax.ShapeDtypeStruct((block.shape[0] // count, block.shape[1]), block.dtype)
    return pl.pallas_call(
        functools.partial(cut_kernel, count),
        out_shape=[part] * count,
        in_specs=[VMEM] + [ANYWHERE] * len(after),
        out_specs=[VMEM] * count,
        compiler_params=pltpu.CompilerParams(vmem_limit_bytes=4 << 20),
        name="cut",
    )(block, *after)


def cut(block, count):
    rows = block.shape[0] // count
    return [block[i * rows : (i + 1) * rows] for i in range(count)]


def cross(block, even, odd):
    count = lax.axis_size("expert")
    pairs = [(i, i ^ (odd if i % 2 else even)) for i in range(count)]
    return lax.ppermute(block, "expert", pairs)


def swap(block, distance):
    count = lax.axis_size("expert")
    return lax.ppermute(block, "expert", [(i, i ^ distance) for i in range(count)])


def spread_step(
    tokens, routes, gate_values, expert_in, expert_out, queries, cached_keys, cached_values, lengths
):
    tok_rows = tokens.shape[0]
    experts_here = lax.axis_size("expert")
    far = [8 * k for k in range(1, experts_here // 8)]
    wide, half = jnp.float32, jnp.bfloat16
    own = label_tokens(tokens, routes, gate_values, experts_here)
    arrived = [swap(own, d) for d in far]
    attended, near_in, near_out = attend_and_fetch(
        queries, cached_keys, cached_values, lengths, expert_in, expert_out
    )

    def gated(parts, results, after=()):
        return run_expert(parts, near_in, near_out, results, after)

    column = stack_rows([own] + arrived, [attended])
    size = column.shape[0]
    pieces = 2
    split = [(size, wide)] + [(size // pieces, half)] * pieces

    def to_pair(block, after=()):
        return [swap(part, 1) for part in cut_rows(block, pieces, after)]

    pair = swap(column, 1)
    side_a = cross(column, 2, 4)
    side_b = cross(pair, 2, 4)
    corner = cross(side_a, 5, 3)
    kept_own, kept_pair = gated([column, pair], [(size, wide)] * 2, [])
    kept_a, *sent_a = gated([side_a] + to_pair(side_a, []), split)
    sum_a = add_parts(kept_a, [swap(part, 1) for part in sent_a])
    got_a = cross(sum_a, 2, 4)
    kept_b, *sent_b = gated([side_b] + to_pair(side_b, []), split, [sum_a])
    sum_b = add_parts(kept_b, [swap(part, 1) for part in sent_b])
    got_b = cross(sum_b, 2, 4)
    kept_c, *sent_c = gated([corner] + to_pair(corner), split, [sum_b])
    sum_c = add_parts(kept_c, [swap(part, 1) for part in sent_c], [])
    shared = add_parts(kept_pair, [got_b], [got_a, sum_c])
    total = kept_own + got_a.astype(wide) + swap(shared, 1).astype(wide)
    bounds = (0, tok_rows, 2 * tok_rows, size)
    returned = []
    for first, last in reversed(list(zip(bounds[:-1], bounds[1:]))):
        returned.append((first, last, swap(sum_c[first:last], 7)))
    sums = {}
    for first, last, block in returned:
        block = total[first:last] + block.astype(wide)
        for k in range(first // tok_rows, last // tok_rows):
            sums[k] = block[k * tok_rows - first : (k + 1) * tok_rows - first]
    final = sums[0]
    for k in (3, 2, 1):
        block = sums[k].astype(half)
        got = [swap(part, far[k - 1]) for part in cut(block, 2 if k == 0 else 1)]
        final = final + (got[0] if len(got) == 1 else jnp.concatenate(got)).astype(wide)
    return final.astype(half), attended.reshape(queries.shape)


def on_device(
    tokens, routes, gate_values, expert_in, expert_out, queries, cached_keys, cached_values, lengths
):
    moe_out = route_experts(tokens, routes, gate_values, expert_in, expert_out)
    attention_out = attend_local(queries, cached_keys, cached_values, lengths)
    return (moe_out, attention_out)


def solution(mesh):
    sizes = dict(mesh.shape)
    spread = sizes["cuts"] == 1 and sizes["expert"] in (8, 16, 32)
    in_specs = (
        P(("groups", "expert", "cuts"), None),
        P(("groups", "expert", "cuts"), None),
        P(("groups", "expert", "cuts"), None),
        P("expert", None, "cuts"),
        P("expert", "cuts", None),
        P(("groups", "expert"), None),
        P(("groups", "expert"), "cuts", None),
        P(("groups", "expert"), "cuts", None),
        P(("groups", "expert")),
    )
    out_specs = (P(("groups", "expert", "cuts"), None), P(("groups", "expert"), None))
    return jax.shard_map(
        spread_step if spread else on_device,
        mesh=mesh,
        in_specs=in_specs,
        out_specs=out_specs,
        check_vma=False,
    )
```

```python
import functools
import math

import jax
import jax.numpy as jnp
from jax import lax
from jax.experimental import pallas as pl
from jax.experimental.pallas import tpu as pltpu
from jax.sharding import PartitionSpec as P

KVH = 4
HD = 128


def attend_local(queries, cached_keys, cached_values, lengths):
    seq_count = queries.shape[0]
    half_span = cached_keys.shape[1]
    group = queries.shape[1] // (KVH * HD)
    first_pos = lax.axis_index("cuts") * half_span
    positions = first_pos + jnp.arange(half_span, dtype=jnp.int32)
    in_cache = (positions[None, :] < lengths[:, None])[:, None, None, :]
    query_blocks = queries.reshape(seq_count, KVH, group, HD)
    key_blocks = cached_keys.reshape(seq_count, half_span, KVH, HD)
    value_blocks = cached_values.reshape(seq_count, half_span, KVH, HD)
    scores = jnp.einsum(
        "skqd,spkd->skqp", query_blocks, key_blocks, preferred_element_type=jnp.float32
    ) / math.sqrt(HD)
    masked = jnp.where(in_cache, scores, jnp.float32(-1e30))
    local_top = jnp.max(masked, axis=-1)
    row_top = lax.pmax(local_top, "cuts")
    weights = jnp.exp(masked - row_top[..., None]).astype(jnp.bfloat16)
    weight_total = jnp.sum(weights.astype(jnp.float32), axis=-1)
    summed = jnp.einsum(
        "skqp,spkd->skqd", weights, value_blocks, preferred_element_type=jnp.float32
    )
    weight_total, summed = lax.psum((weight_total, summed), "cuts")
    return (
        (summed / weight_total[..., None]).reshape(seq_count, KVH * group * HD).astype(jnp.bfloat16)
    )


def route_experts(tokens, routes, gate_values, expert_in, expert_out):
    tok_rows, width = tokens.shape
    top_count = routes.shape[1]
    experts_here = lax.axis_size("expert")
    capacity = min(tok_rows, 2 * tok_rows * top_count // experts_here)
    expert_ids = jnp.arange(experts_here, dtype=jnp.int32)
    chosen = routes[:, :, None] == expert_ids[None, None, :]
    member = jnp.sum(chosen, axis=1).astype(jnp.float32)
    gate_here = jnp.sum(
        jnp.where(chosen, gate_values.astype(jnp.float32)[:, :, None], jnp.float32(0.0)), axis=1
    )
    earlier = (jnp.arange(tok_rows)[:, None] > jnp.arange(tok_rows)[None, :]).astype(jnp.float32)
    slot_index = jnp.dot(earlier, member, precision=lax.Precision.HIGHEST)
    placed = (slot_index[:, :, None] == jnp.arange(capacity, dtype=jnp.float32)[None, None, :]) & (
        member[:, :, None] > 0.5
    )
    send_matrix = placed.astype(jnp.bfloat16).reshape(tok_rows, experts_here * capacity)
    combine_matrix = (
        (placed.astype(jnp.float32) * gate_here[:, :, None])
        .astype(jnp.bfloat16)
        .reshape(tok_rows, experts_here * capacity)
    )
    outgoing = jnp.einsum("tr,td->rd", send_matrix, tokens, preferred_element_type=jnp.float32)
    outgoing = outgoing.astype(jnp.bfloat16).reshape(experts_here, capacity, width)
    arrived = lax.all_to_all(outgoing, "expert", split_axis=0, concat_axis=0, tiled=True)
    slot_rows = arrived.reshape(-1, width)
    hidden = jax.nn.silu(
        jnp.dot(
            lax.all_gather(slot_rows, "cuts", axis=0, tiled=True),
            expert_in[0],
            preferred_element_type=jnp.float32,
        )
    ).astype(jnp.bfloat16)
    produced = lax.psum_scatter(
        jnp.dot(hidden, expert_out[0], preferred_element_type=jnp.float32),
        "cuts",
        scatter_dimension=0,
        tiled=True,
    ).astype(jnp.bfloat16)
    returned = lax.all_to_all(
        produced.reshape(arrived.shape), "expert", split_axis=0, concat_axis=0, tiled=True
    )
    combined = jnp.dot(
        combine_matrix,
        returned.reshape(experts_here * capacity, width),
        preferred_element_type=jnp.float32,
    )
    return combined.astype(jnp.bfloat16)


LANES = 128
VMEM = pl.BlockSpec(memory_space=pltpu.VMEM)
SMEM = pl.BlockSpec(memory_space=pltpu.SMEM)
ANYWHERE = pl.BlockSpec(memory_space=pl.ANY)
HBM = pl.BlockSpec(memory_space=pltpu.HBM)


def far_off(x):
    return pltpu.with_memory_space_constraint(x, pltpu.HBM)


def label_kernel(tokens_hbm, routes_hbm, gates_hbm, own_ref, routes_ref, gates_ref, sems):
    tok_rows, width = tokens_hbm.shape
    lanes = own_ref.shape[1] - width
    copies = [
        pltpu.make_async_copy(tokens_hbm, own_ref.at[:, pl.ds(0, width)], sems.at[0]),
        pltpu.make_async_copy(routes_hbm, routes_ref, sems.at[1]),
        pltpu.make_async_copy(gates_hbm, gates_ref, sems.at[2]),
    ]
    for copy in copies:
        copy.start()
    copies[1].wait()
    copies[2].wait()
    routes = routes_ref[...]
    gates = gates_ref[...].astype(jnp.float32)
    ids = lax.broadcasted_iota(jnp.int32, (lanes, tok_rows), 0)
    spread = jnp.zeros((lanes, tok_rows), jnp.float32)
    for k in range(routes.shape[0]):
        spread += jnp.where(ids == routes[k : k + 1, :], gates[k : k + 1, :], 0.0)
    places = (tok_rows, tok_rows)
    same = lax.broadcasted_iota(jnp.int32, places, 0) == lax.broadcasted_iota(jnp.int32, places, 1)
    turned = lax.dot_general(
        same.astype(jnp.bfloat16),
        spread.astype(jnp.bfloat16),
        (((1,), (1,)), ((), ())),
        preferred_element_type=jnp.float32,
    )
    own_ref[:, width:] = turned.astype(own_ref.dtype)
    copies[0].wait()


def label_tokens(tokens, routes, gate_values, experts):
    tok_rows, width = tokens.shape
    lanes = -(-experts // LANES) * LANES
    return pl.pallas_call(
        label_kernel,
        out_shape=jax.ShapeDtypeStruct((tok_rows, width + lanes), jnp.bfloat16),
        in_specs=[HBM] * 3,
        out_specs=VMEM,
        scratch_shapes=[
            pltpu.VMEM(routes.shape[::-1], routes.dtype),
            pltpu.VMEM(gate_values.shape[::-1], gate_values.dtype),
            pltpu.SemaphoreType.DMA((3,)),
        ],
        compiler_params=pltpu.CompilerParams(vmem_limit_bytes=4 << 20),
        name="label",
    )(far_off(tokens), far_off(routes.T), far_off(gate_values.T))


def attend_kernel(
    lengths_ref, query_ref, key_hbm, value_hbm, in_hbm, proj_hbm, out_ref, in_ref, proj_ref,
    key_ref, value_ref, sems
):
    pairs = ((key_hbm, key_ref), (value_hbm, value_ref), (in_hbm, in_ref), (proj_hbm, proj_ref))
    copies = [pltpu.make_async_copy(a, b, sems.at[i]) for i, (a, b) in enumerate(pairs)]
    for copy in copies:
        copy.start()
    head_count = query_ref.shape[1] // HD
    span = key_ref.shape[0]
    group = head_count // KVH
    query = query_ref[...].astype(jnp.float32)
    heads = [query[:, i * HD : (i + 1) * HD] for i in range(head_count)]
    live = lax.broadcasted_iota(jnp.int32, (group, span), 1) < lengths_ref[0]
    copies[0].wait()
    for k in range(KVH):
        rows = slice(k * group, (k + 1) * group)
        columns = slice(k * HD, (k + 1) * HD)
        scores = lax.dot_general(
            jnp.concatenate(heads[rows], axis=0).astype(jnp.bfloat16),
            key_ref[:, columns],
            (((1,), (1,)), ((), ())),
            preferred_element_type=jnp.float32,
        ) * (1.0 / math.sqrt(HD))
        masked = jnp.where(live, scores, jnp.float32(-1e30))
        top = jnp.max(masked, axis=1, keepdims=True)
        weights = jnp.exp(masked - top).astype(jnp.bfloat16)
        total = jnp.sum(weights.astype(jnp.float32), axis=1, keepdims=True)
        if k == 0:
            copies[1].wait()
        summed = jnp.dot(weights, value_ref[:, columns], preferred_element_type=jnp.float32)
        out_ref[rows, :] = (summed / total).astype(out_ref.dtype)
    copies[2].wait()
    copies[3].wait()


def attend_and_fetch(queries, cached_keys, cached_values, lengths, expert_in, expert_out):
    width = queries.shape[1]
    head_count = width // HD
    span = cached_keys.shape[1]
    attended, near_in, near_out = pl.pallas_call(
        attend_kernel,
        out_shape=[
            jax.ShapeDtypeStruct((head_count, HD), jnp.bfloat16),
            pltpu.VMEM(expert_in.shape[1:], jnp.bfloat16),
            pltpu.VMEM(expert_out.shape[1:], jnp.bfloat16),
        ],
        in_specs=[SMEM, VMEM] + [HBM] * 4,
        out_specs=[VMEM] * 3,
        scratch_shapes=[
            pltpu.VMEM(cached_keys.shape[1:], jnp.bfloat16),
            pltpu.VMEM(cached_values.shape[1:], jnp.bfloat16),
            pltpu.SemaphoreType.DMA((4,)),
        ],
        compiler_params=pltpu.CompilerParams(vmem_limit_bytes=14 << 20),
        cost_estimate=pl.CostEstimate(
            flops=4 * head_count * HD * span,
            bytes_accessed=4 * span * KVH * HD + 4 * expert_in.size + 4 * expert_out.size,
            transcendentals=head_count * span,
        ),
        name="attention",
    )(
        lengths,
        queries,
        *(far_off(a[0]) for a in (cached_keys, cached_values, expert_in, expert_out)),
    )
    return attended, near_in, near_out


def stack_kernel(part_count, *refs):
    parts, out_ref = refs[:part_count], refs[-1]
    size = parts[0].shape[0]
    for i, part in enumerate(parts):
        out_ref[i * size : (i + 1) * size, :] = part[...]


def stack_rows(parts, after=()):
    size, width = parts[0].shape
    return pl.pallas_call(
        functools.partial(stack_kernel, len(parts)),
        out_shape=jax.ShapeDtypeStruct((size * len(parts), width), parts[0].dtype),
        in_specs=[VMEM] * len(parts) + [ANYWHERE] * len(after),
        out_specs=VMEM,
        compiler_params=pltpu.CompilerParams(vmem_limit_bytes=4 << 20),
        name="stack",
    )(*parts, *after)


def expert_kernel(part_count, after_count, *refs):
    parts, (in_ref, proj_ref), results = (
        refs[:part_count], refs[part_count : part_count + 2], refs[part_count + 2 + after_count :]
    )
    width = in_ref.shape[0]
    rows = jnp.concatenate([part[:, :width] for part in parts], axis=0)
    gates = jnp.concatenate([part[:, width:] for part in parts], axis=0).astype(jnp.float32)
    lane = lax.broadcasted_iota(jnp.int32, gates.shape, 1)
    gate = jnp.sum(jnp.where(lane == lax.axis_index("expert"), gates, 0.0), axis=1, keepdims=True)
    pre = jnp.dot(rows, in_ref[...], preferred_element_type=jnp.float32)
    hidden = (pre / (1.0 + jnp.exp(-pre))).astype(jnp.bfloat16)
    produced = jnp.dot(hidden, proj_ref[...], preferred_element_type=jnp.float32) * gate
    first = 0
    for result in results:
        size = result.shape[0]
        result[...] = produced[first : first + size].astype(result.dtype)
        first += size


def run_expert(parts, near_in, near_out, results, after):
    count = sum(part.shape[0] for part in parts)
    width, units = near_in.shape
    return pl.pallas_call(
        functools.partial(expert_kernel, len(parts), len(after)),
        out_shape=[jax.ShapeDtypeStruct((size, width), kind) for size, kind in results],
        in_specs=[VMEM] * (len(parts) + 2) + [ANYWHERE] * len(after),
        out_specs=[VMEM] * len(results),
        compiler_params=pltpu.CompilerParams(vmem_limit_bytes=14 << 20),
        cost_estimate=pl.CostEstimate(
            flops=4 * count * width * units,
            bytes_accessed=6 * count * width,
            transcendentals=count * units,
        ),
        name="expert",
    )(*parts, hold(near_in), hold(near_out), *after)


def hold(x):
    return pltpu.with_memory_space_constraint(x, pltpu.VMEM)


def add_kernel(part_count, *refs):
    kept_ref, parts, result_ref = refs[0], refs[1 : part_count + 1], refs[-1]
    back = jnp.concatenate([part[...] for part in parts], axis=0).astype(jnp.float32)
    result_ref[...] = (kept_ref[...] + back).astype(result_ref.dtype)


def add_parts(kept, parts, after=()):
    return pl.pallas_call(
        functools.partial(add_kernel, len(parts)),
        out_shape=jax.ShapeDtypeStruct(kept.shape, parts[0].dtype),
        in_specs=[VMEM] * (len(parts) + 1) + [ANYWHERE] * len(after),
        out_specs=VMEM,
        compiler_params=pltpu.CompilerParams(vmem_limit_bytes=6 << 20),
        name="add",
    )(kept, *parts, *after)


def finish_kernel(first, total_ref, block_ref, *part_refs):
    rows = part_refs[0].shape[0]
    for i, part_ref in enumerate(part_refs):
        at = slice(first + i * rows, first + (i + 1) * rows)
        block = block_ref[i * rows : (i + 1) * rows, :].astype(jnp.float32)
        part_ref[...] = (total_ref[at, :] + block).astype(part_ref.dtype)


def finish_rows(total, block, first, count):
    part = jax.ShapeDtypeStruct((block.shape[0] // count, block.shape[1]), block.dtype)
    return pl.pallas_call(
        functools.partial(finish_kernel, first),
        out_shape=[part] * count,
        in_specs=[VMEM] * 2,
        out_specs=[VMEM] * count,
        compiler_params=pltpu.CompilerParams(vmem_limit_bytes=4 << 20),
        name="finish",
    )(total, block)


def cut_kernel(count, block_ref, *refs):
    rows = block_ref.shape[0] // count
    for i, part_ref in enumerate(refs[-count:]):
        part_ref[...] = block_ref[i * rows : (i + 1) * rows, :]


def cut_rows(block, count, after=()):
    part = jax.ShapeDtypeStruct((block.shape[0] // count, block.shape[1]), block.dtype)
    return pl.pallas_call(
        functools.partial(cut_kernel, count),
        out_shape=[part] * count,
        in_specs=[VMEM] + [ANYWHERE] * len(after),
        out_specs=[VMEM] * count,
        compiler_params=pltpu.CompilerParams(vmem_limit_bytes=4 << 20),
        name="cut",
    )(block, *after)


def cut(block, count):
    rows = block.shape[0] // count
    return [block[i * rows : (i + 1) * rows] for i in range(count)]


def cross(block, even, odd):
    count = lax.axis_size("expert")
    pairs = [(i, i ^ (odd if i % 2 else even)) for i in range(count)]
    return lax.ppermute(block, "expert", pairs)


def swap(block, distance):
    count = lax.axis_size("expert")
    return lax.ppermute(block, "expert", [(i, i ^ distance) for i in range(count)])


def spread_step(
    tokens, routes, gate_values, expert_in, expert_out, queries, cached_keys, cached_values, lengths
):
    tok_rows = tokens.shape[0]
    experts_here = lax.axis_size("expert")
    far = [8 * k for k in range(1, experts_here // 8)]
    wide, half = jnp.float32, jnp.bfloat16
    own = label_tokens(tokens, routes, gate_values, experts_here)
    arrived = [swap(own, d) for d in far]
    attended, near_in, near_out = attend_and_fetch(
        queries, cached_keys, cached_values, lengths, expert_in, expert_out
    )

    def gated(parts, results, after=()):
        return run_expert(parts, near_in, near_out, results, after)

    column = stack_rows([own] + arrived, [attended])
    size = column.shape[0]
    pieces = 2
    split = [(size, wide)] + [(size // pieces, half)] * pieces

    def to_pair(block, after=()):
        return [swap(part, 1) for part in cut_rows(block, pieces, after)]

    pair = swap(column, 1)
    side_a = cross(column, 2, 4)
    side_b = cross(pair, 2, 4)
    corner = cross(side_a, 5, 3)
    kept_own, kept_pair = gated([column, pair], [(size, wide)] * 2, [])
    kept_a, *sent_a = gated([side_a] + to_pair(side_a, []), split)
    sum_a = add_parts(kept_a, [swap(part, 1) for part in sent_a])
    got_a = cross(sum_a, 2, 4)
    kept_b, *sent_b = gated([side_b] + to_pair(side_b, [kept_a]), split, [sum_a])
    sum_b = add_parts(kept_b, [swap(part, 1) for part in sent_b])
    got_b = cross(sum_b, 2, 4)
    kept_c, *sent_c = gated([corner] + to_pair(corner), split, [sum_b])
    sum_c = add_parts(kept_c, [swap(part, 1) for part in sent_c], [])
    shared = add_parts(kept_pair, [got_b], [got_a, sum_c])
    total = kept_own + got_a.astype(wide) + swap(shared, 1).astype(wide)
    bounds = (0, tok_rows, 2 * tok_rows, size)
    returned = []
    for first, last in reversed(list(zip(bounds[:-1], bounds[1:]))):
        returned.append((first, last, swap(sum_c[first:last], 7)))
    sums = {}
    for first, last, block in returned:
        block = total[first:last] + block.astype(wide)
        for k in range(first // tok_rows, last // tok_rows):
            sums[k] = block[k * tok_rows - first : (k + 1) * tok_rows - first]
    final = sums[0]
    for k in (3, 2, 1):
        block = sums[k].astype(half)
        got = [swap(part, far[k - 1]) for part in cut(block, 2 if k == 0 else 1)]
        final = final + (got[0] if len(got) == 1 else jnp.concatenate(got)).astype(wide)
    return final.astype(half), attended.reshape(queries.shape)


def on_device(
    tokens, routes, gate_values, expert_in, expert_out, queries, cached_keys, cached_values, lengths
):
    moe_out = route_experts(tokens, routes, gate_values, expert_in, expert_out)
    attention_out = attend_local(queries, cached_keys, cached_values, lengths)
    return (moe_out, attention_out)


def solution(mesh):
    sizes = dict(mesh.shape)
    spread = sizes["cuts"] == 1 and sizes["expert"] in (8, 16, 32)
    in_specs = (
        P(("groups", "expert", "cuts"), None),
        P(("groups", "expert", "cuts"), None),
        P(("groups", "expert", "cuts"), None),
        P("expert", None, "cuts"),
        P("expert", "cuts", None),
        P(("groups", "expert"), None),
        P(("groups", "expert"), "cuts", None),
        P(("groups", "expert"), "cuts", None),
        P(("groups", "expert")),
    )
    out_specs = (P(("groups", "expert", "cuts"), None), P(("groups", "expert"), None))
    return jax.shard_map(
        spread_step if spread else on_device,
        mesh=mesh,
        in_specs=in_specs,
        out_specs=out_specs,
        check_vma=False,
    )
```

```python
import functools
import math

import jax
import jax.numpy as jnp
from jax import lax
from jax.experimental import pallas as pl
from jax.experimental.pallas import tpu as pltpu
from jax.sharding import PartitionSpec as P

KVH = 4
HD = 128


def attend_local(queries, cached_keys, cached_values, lengths):
    seq_count = queries.shape[0]
    half_span = cached_keys.shape[1]
    group = queries.shape[1] // (KVH * HD)
    first_pos = lax.axis_index("cuts") * half_span
    positions = first_pos + jnp.arange(half_span, dtype=jnp.int32)
    in_cache = (positions[None, :] < lengths[:, None])[:, None, None, :]
    query_blocks = queries.reshape(seq_count, KVH, group, HD)
    key_blocks = cached_keys.reshape(seq_count, half_span, KVH, HD)
    value_blocks = cached_values.reshape(seq_count, half_span, KVH, HD)
    scores = jnp.einsum(
        "skqd,spkd->skqp", query_blocks, key_blocks, preferred_element_type=jnp.float32
    ) / math.sqrt(HD)
    masked = jnp.where(in_cache, scores, jnp.float32(-1e30))
    local_top = jnp.max(masked, axis=-1)
    row_top = lax.pmax(local_top, "cuts")
    weights = jnp.exp(masked - row_top[..., None]).astype(jnp.bfloat16)
    weight_total = jnp.sum(weights.astype(jnp.float32), axis=-1)
    summed = jnp.einsum(
        "skqp,spkd->skqd", weights, value_blocks, preferred_element_type=jnp.float32
    )
    weight_total, summed = lax.psum((weight_total, summed), "cuts")
    return (
        (summed / weight_total[..., None]).reshape(seq_count, KVH * group * HD).astype(jnp.bfloat16)
    )


def route_experts(tokens, routes, gate_values, expert_in, expert_out):
    tok_rows, width = tokens.shape
    top_count = routes.shape[1]
    experts_here = lax.axis_size("expert")
    capacity = min(tok_rows, 2 * tok_rows * top_count // experts_here)
    expert_ids = jnp.arange(experts_here, dtype=jnp.int32)
    chosen = routes[:, :, None] == expert_ids[None, None, :]
    member = jnp.sum(chosen, axis=1).astype(jnp.float32)
    gate_here = jnp.sum(
        jnp.where(chosen, gate_values.astype(jnp.float32)[:, :, None], jnp.float32(0.0)), axis=1
    )
    earlier = (jnp.arange(tok_rows)[:, None] > jnp.arange(tok_rows)[None, :]).astype(jnp.float32)
    slot_index = jnp.dot(earlier, member, precision=lax.Precision.HIGHEST)
    placed = (slot_index[:, :, None] == jnp.arange(capacity, dtype=jnp.float32)[None, None, :]) & (
        member[:, :, None] > 0.5
    )
    send_matrix = placed.astype(jnp.bfloat16).reshape(tok_rows, experts_here * capacity)
    combine_matrix = (
        (placed.astype(jnp.float32) * gate_here[:, :, None])
        .astype(jnp.bfloat16)
        .reshape(tok_rows, experts_here * capacity)
    )
    outgoing = jnp.einsum("tr,td->rd", send_matrix, tokens, preferred_element_type=jnp.float32)
    outgoing = outgoing.astype(jnp.bfloat16).reshape(experts_here, capacity, width)
    arrived = lax.all_to_all(outgoing, "expert", split_axis=0, concat_axis=0, tiled=True)
    slot_rows = arrived.reshape(-1, width)
    hidden = jax.nn.silu(
        jnp.dot(
            lax.all_gather(slot_rows, "cuts", axis=0, tiled=True),
            expert_in[0],
            preferred_element_type=jnp.float32,
        )
    ).astype(jnp.bfloat16)
    produced = lax.psum_scatter(
        jnp.dot(hidden, expert_out[0], preferred_element_type=jnp.float32),
        "cuts",
        scatter_dimension=0,
        tiled=True,
    ).astype(jnp.bfloat16)
    returned = lax.all_to_all(
        produced.reshape(arrived.shape), "expert", split_axis=0, concat_axis=0, tiled=True
    )
    combined = jnp.dot(
        combine_matrix,
        returned.reshape(experts_here * capacity, width),
        preferred_element_type=jnp.float32,
    )
    return combined.astype(jnp.bfloat16)


LANES = 128
VMEM = pl.BlockSpec(memory_space=pltpu.VMEM)
SMEM = pl.BlockSpec(memory_space=pltpu.SMEM)
ANYWHERE = pl.BlockSpec(memory_space=pl.ANY)
HBM = pl.BlockSpec(memory_space=pltpu.HBM)


def far_off(x):
    return pltpu.with_memory_space_constraint(x, pltpu.HBM)


def label_kernel(tokens_hbm, routes_hbm, gates_hbm, own_ref, routes_ref, gates_ref, sems):
    tok_rows, width = tokens_hbm.shape
    lanes = own_ref.shape[1] - width
    copies = [
        pltpu.make_async_copy(tokens_hbm, own_ref.at[:, pl.ds(0, width)], sems.at[0]),
        pltpu.make_async_copy(routes_hbm, routes_ref, sems.at[1]),
        pltpu.make_async_copy(gates_hbm, gates_ref, sems.at[2]),
    ]
    for copy in copies:
        copy.start()
    copies[1].wait()
    copies[2].wait()
    routes = routes_ref[...]
    gates = gates_ref[...].astype(jnp.float32)
    ids = lax.broadcasted_iota(jnp.int32, (lanes, tok_rows), 0)
    spread = jnp.zeros((lanes, tok_rows), jnp.float32)
    for k in range(routes.shape[0]):
        spread += jnp.where(ids == routes[k : k + 1, :], gates[k : k + 1, :], 0.0)
    places = (tok_rows, tok_rows)
    same = lax.broadcasted_iota(jnp.int32, places, 0) == lax.broadcasted_iota(jnp.int32, places, 1)
    turned = lax.dot_general(
        same.astype(jnp.bfloat16),
        spread.astype(jnp.bfloat16),
        (((1,), (1,)), ((), ())),
        preferred_element_type=jnp.float32,
    )
    own_ref[:, width:] = turned.astype(own_ref.dtype)
    copies[0].wait()


def label_tokens(tokens, routes, gate_values, experts):
    tok_rows, width = tokens.shape
    lanes = -(-experts // LANES) * LANES
    return pl.pallas_call(
        label_kernel,
        out_shape=jax.ShapeDtypeStruct((tok_rows, width + lanes), jnp.bfloat16),
        in_specs=[HBM] * 3,
        out_specs=VMEM,
        scratch_shapes=[
            pltpu.VMEM(routes.shape[::-1], routes.dtype),
            pltpu.VMEM(gate_values.shape[::-1], gate_values.dtype),
            pltpu.SemaphoreType.DMA((3,)),
        ],
        compiler_params=pltpu.CompilerParams(vmem_limit_bytes=4 << 20),
        name="label",
    )(far_off(tokens), far_off(routes.T), far_off(gate_values.T))


def attend_kernel(
    lengths_ref, query_hbm, key_hbm, value_hbm, out_ref, query_ref, key_ref, value_ref, sems
):
    pairs = ((query_hbm, query_ref), (key_hbm, key_ref), (value_hbm, value_ref))
    copies = [pltpu.make_async_copy(a, b, sems.at[i]) for i, (a, b) in enumerate(pairs)]
    for copy in copies:
        copy.start()
    head_count = query_ref.shape[1] // HD
    span = key_ref.shape[0]
    group = head_count // KVH
    live = lax.broadcasted_iota(jnp.int32, (group, span), 1) < lengths_ref[0]
    copies[0].wait()
    query = query_ref[...].astype(jnp.float32)
    heads = [query[:, i * HD : (i + 1) * HD] for i in range(head_count)]
    copies[1].wait()
    for k in range(KVH):
        rows = slice(k * group, (k + 1) * group)
        columns = slice(k * HD, (k + 1) * HD)
        scores = lax.dot_general(
            jnp.concatenate(heads[rows], axis=0).astype(jnp.bfloat16),
            key_ref[:, columns],
            (((1,), (1,)), ((), ())),
            preferred_element_type=jnp.float32,
        ) * (1.0 / math.sqrt(HD))
        masked = jnp.where(live, scores, jnp.float32(-1e30))
        top = jnp.max(masked, axis=1, keepdims=True)
        weights = jnp.exp(masked - top).astype(jnp.bfloat16)
        total = jnp.sum(weights.astype(jnp.float32), axis=1, keepdims=True)
        if k == 0:
            copies[2].wait()
        summed = jnp.dot(weights, value_ref[:, columns], preferred_element_type=jnp.float32)
        out_ref[rows, :] = (summed / total).astype(out_ref.dtype)


def attend_whole(queries, cached_keys, cached_values, lengths):
    width = queries.shape[1]
    head_count = width // HD
    span = cached_keys.shape[1]
    return pl.pallas_call(
        attend_kernel,
        out_shape=jax.ShapeDtypeStruct((head_count, HD), jnp.bfloat16),
        in_specs=[SMEM] + [HBM] * 3,
        out_specs=VMEM,
        scratch_shapes=[
            pltpu.VMEM(queries.shape, jnp.bfloat16),
            pltpu.VMEM(cached_keys.shape[1:], jnp.bfloat16),
            pltpu.VMEM(cached_values.shape[1:], jnp.bfloat16),
            pltpu.SemaphoreType.DMA((3,)),
        ],
        compiler_params=pltpu.CompilerParams(vmem_limit_bytes=8 << 20),
        cost_estimate=pl.CostEstimate(
            flops=4 * head_count * HD * span,
            bytes_accessed=4 * span * KVH * HD,
            transcendentals=head_count * span,
        ),
        name="attention",
    )(lengths, far_off(queries), far_off(cached_keys[0]), far_off(cached_values[0]))


def fetch_kernel(in_hbm, proj_hbm, *refs):
    in_ref, proj_ref, mark_ref, sems = refs[-4:]
    copies = [
        pltpu.make_async_copy(in_hbm, in_ref, sems.at[0]),
        pltpu.make_async_copy(proj_hbm, proj_ref, sems.at[1]),
    ]
    for copy in copies:
        copy.start()
    mark_ref[...] = jnp.zeros_like(mark_ref)
    for copy in copies:
        copy.wait()


def fetch_expert(expert_in, expert_out, after=()):
    return pl.pallas_call(
        fetch_kernel,
        out_shape=[
            pltpu.VMEM(expert_in.shape[1:], jnp.bfloat16),
            pltpu.VMEM(expert_out.shape[1:], jnp.bfloat16),
            jax.ShapeDtypeStruct((8, LANES), jnp.float32),
        ],
        in_specs=[HBM] * 2 + [ANYWHERE] * len(after),
        out_specs=[VMEM] * 3,
        scratch_shapes=[pltpu.SemaphoreType.DMA((2,))],
        compiler_params=pltpu.CompilerParams(vmem_limit_bytes=14 << 20),
        cost_estimate=pl.CostEstimate(
            flops=0, bytes_accessed=2 * expert_in.size + 2 * expert_out.size, transcendentals=0
        ),
        name="fetch",
    )(far_off(expert_in[0]), far_off(expert_out[0]), *after)


def stack_kernel(part_count, *refs):
    parts, out_ref = refs[:part_count], refs[-1]
    size = parts[0].shape[0]
    for i, part in enumerate(parts):
        out_ref[i * size : (i + 1) * size, :] = part[...]


def stack_rows(parts, after=()):
    size, width = parts[0].shape
    return pl.pallas_call(
        functools.partial(stack_kernel, len(parts)),
        out_shape=jax.ShapeDtypeStruct((size * len(parts), width), parts[0].dtype),
        in_specs=[VMEM] * len(parts) + [ANYWHERE] * len(after),
        out_specs=VMEM,
        compiler_params=pltpu.CompilerParams(vmem_limit_bytes=4 << 20),
        name="stack",
    )(*parts, *after)


def expert_kernel(part_count, after_count, *refs):
    parts, (in_ref, proj_ref), results = (
        refs[:part_count], refs[part_count : part_count + 2], refs[part_count + 2 + after_count :]
    )
    width = in_ref.shape[0]
    rows = jnp.concatenate([part[:, :width] for part in parts], axis=0)
    gates = jnp.concatenate([part[:, width:] for part in parts], axis=0).astype(jnp.float32)
    lane = lax.broadcasted_iota(jnp.int32, gates.shape, 1)
    gate = jnp.sum(jnp.where(lane == lax.axis_index("expert"), gates, 0.0), axis=1, keepdims=True)
    pre = jnp.dot(rows, in_ref[...], preferred_element_type=jnp.float32)
    hidden = (pre / (1.0 + jnp.exp(-pre))).astype(jnp.bfloat16)
    produced = jnp.dot(hidden, proj_ref[...], preferred_element_type=jnp.float32) * gate
    first = 0
    for result in results:
        size = result.shape[0]
        result[...] = produced[first : first + size].astype(result.dtype)
        first += size


def run_expert(parts, near_in, near_out, results, after):
    count = sum(part.shape[0] for part in parts)
    width, units = near_in.shape
    return pl.pallas_call(
        functools.partial(expert_kernel, len(parts), len(after)),
        out_shape=[jax.ShapeDtypeStruct((size, width), kind) for size, kind in results],
        in_specs=[VMEM] * (len(parts) + 2) + [ANYWHERE] * len(after),
        out_specs=[VMEM] * len(results),
        compiler_params=pltpu.CompilerParams(vmem_limit_bytes=14 << 20),
        cost_estimate=pl.CostEstimate(
            flops=4 * count * width * units,
            bytes_accessed=6 * count * width,
            transcendentals=count * units,
        ),
        name="expert",
    )(*parts, hold(near_in), hold(near_out), *after)


def hold(x):
    return pltpu.with_memory_space_constraint(x, pltpu.VMEM)


def add_kernel(part_count, *refs):
    kept_ref, parts, result_ref = refs[0], refs[1 : part_count + 1], refs[-1]
    back = jnp.concatenate([part[...] for part in parts], axis=0).astype(jnp.float32)
    result_ref[...] = (kept_ref[...] + back).astype(result_ref.dtype)


def add_parts(kept, parts, after=()):
    return pl.pallas_call(
        functools.partial(add_kernel, len(parts)),
        out_shape=jax.ShapeDtypeStruct(kept.shape, parts[0].dtype),
        in_specs=[VMEM] * (len(parts) + 1) + [ANYWHERE] * len(after),
        out_specs=VMEM,
        compiler_params=pltpu.CompilerParams(vmem_limit_bytes=6 << 20),
        name="add",
    )(kept, *parts, *after)


def finish_kernel(first, total_ref, block_ref, *part_refs):
    rows = part_refs[0].shape[0]
    for i, part_ref in enumerate(part_refs):
        at = slice(first + i * rows, first + (i + 1) * rows)
        block = block_ref[i * rows : (i + 1) * rows, :].astype(jnp.float32)
        part_ref[...] = (total_ref[at, :] + block).astype(part_ref.dtype)


def finish_rows(total, block, first, count):
    part = jax.ShapeDtypeStruct((block.shape[0] // count, block.shape[1]), block.dtype)
    return pl.pallas_call(
        functools.partial(finish_kernel, first),
        out_shape=[part] * count,
        in_specs=[VMEM] * 2,
        out_specs=[VMEM] * count,
        compiler_params=pltpu.CompilerParams(vmem_limit_bytes=4 << 20),
        name="finish",
    )(total, block)


def cut_kernel(count, block_ref, *refs):
    rows = block_ref.shape[0] // count
    for i, part_ref in enumerate(refs[-count:]):
        part_ref[...] = block_ref[i * rows : (i + 1) * rows, :]


def cut_rows(block, count, after=()):
    part = jax.ShapeDtypeStruct((block.shape[0] // count, block.shape[1]), block.dtype)
    return pl.pallas_call(
        functools.partial(cut_kernel, count),
        out_shape=[part] * count,
        in_specs=[VMEM] + [ANYWHERE] * len(after),
        out_specs=[VMEM] * count,
        compiler_params=pltpu.CompilerParams(vmem_limit_bytes=4 << 20),
        name="cut",
    )(block, *after)


def cut(block, count):
    rows = block.shape[0] // count
    return [block[i * rows : (i + 1) * rows] for i in range(count)]


def cross(block, even, odd):
    count = lax.axis_size("expert")
    pairs = [(i, i ^ (odd if i % 2 else even)) for i in range(count)]
    return lax.ppermute(block, "expert", pairs)


def swap(block, distance):
    count = lax.axis_size("expert")
    return lax.ppermute(block, "expert", [(i, i ^ distance) for i in range(count)])


def spread_step(
    tokens, routes, gate_values, expert_in, expert_out, queries, cached_keys, cached_values, lengths
):
    tok_rows = tokens.shape[0]
    experts_here = lax.axis_size("expert")
    far = [8 * k for k in range(experts_here // 8 - 1, 0, -1)]
    wide, half = jnp.float32, jnp.bfloat16
    own = label_tokens(tokens, routes, gate_values, experts_here)
    arrived = [swap(own, d) for d in far]
    attended = attend_whole(queries, cached_keys, cached_values, lengths)
    column = stack_rows([own] + arrived, [attended])
    near_in, near_out, mark = fetch_expert(expert_in, expert_out, [column])

    def gated(parts, results, after=()):
        return run_expert(parts, near_in, near_out, results, after)

    size = column.shape[0]
    pieces = 2
    split = [(size, wide)] + [(size // pieces, half)] * pieces

    def to_pair(block, after=()):
        return [swap(part, 1) for part in cut_rows(block, pieces, after)]

    pair = swap(column, 1)
    side_a = cross(column, 2, 4)
    side_b = cross(pair, 2, 4)
    corner = cross(side_a, 5, 3)
    kept_own, kept_pair = gated([column, pair], [(size, wide)] * 2, [])
    kept_a, *sent_a = gated([side_a] + to_pair(side_a, [mark]), split)
    sum_a = add_parts(kept_a, [swap(part, 1) for part in sent_a])
    got_a = cross(sum_a, 2, 4)
    kept_b, *sent_b = gated([side_b] + to_pair(side_b, [kept_a]), split, [sum_a])
    sum_b = add_parts(kept_b, [swap(part, 1) for part in sent_b])
    got_b = cross(sum_b, 2, 4)
    kept_c, *sent_c = gated([corner] + to_pair(corner), split, [sum_b])
    sum_c = add_parts(kept_c, [swap(part, 1) for part in sent_c], [])
    shared = add_parts(kept_pair, [got_b], [got_a, sum_c])
    total = kept_own + got_a.astype(wide) + swap(shared, 1).astype(wide)
    returned = []
    for first, last in ((tok_rows, 3 * tok_rows), (3 * tok_rows, size), (0, tok_rows)):
        returned.append((first, last, swap(sum_c[first:last], 7)))
    sums = {}
    for first, last, block in returned:
        block = total[first:last] + block.astype(wide)
        for k in range(first // tok_rows, last // tok_rows):
            sums[k] = block[k * tok_rows - first : (k + 1) * tok_rows - first]
    final = sums[0]
    for k in (1, 2, 3):
        block = sums[k].astype(half)
        got = [swap(part, far[k - 1]) for part in cut(block, 2 if k == 0 else 1)]
        final = final + (got[0] if len(got) == 1 else jnp.concatenate(got)).astype(wide)
    return final.astype(half), attended.reshape(queries.shape)


def on_device(
    tokens, routes, gate_values, expert_in, expert_out, queries, cached_keys, cached_values, lengths
):
    moe_out = route_experts(tokens, routes, gate_values, expert_in, expert_out)
    attention_out = attend_local(queries, cached_keys, cached_values, lengths)
    return (moe_out, attention_out)


def solution(mesh):
    sizes = dict(mesh.shape)
    spread = sizes["cuts"] == 1 and sizes["expert"] == 32
    in_specs = (
        P(("groups", "expert", "cuts"), None),
        P(("groups", "expert", "cuts"), None),
        P(("groups", "expert", "cuts"), None),
        P("expert", None, "cuts"),
        P("expert", "cuts", None),
        P(("groups", "expert"), None),
        P(("groups", "expert"), "cuts", None),
        P(("groups", "expert"), "cuts", None),
        P(("groups", "expert")),
    )
    out_specs = (P(("groups", "expert", "cuts"), None), P(("groups", "expert"), None))
    return jax.shard_map(
        spread_step if spread else on_device,
        mesh=mesh,
        in_specs=in_specs,
        out_specs=out_specs,
        check_vma=False,
    )
```
